256 devices in a mesh: dom: 64 (over y, z, core), feat: 4 (over x).
Axes of the slice: x: 4, y: 4, z: 8, core: 2. Of those that a mesh axis runs over, the one named last changes fastest.
Arguments:
- features: bfloat16 [131072, 256], P('dom', 'feat'), may hold values from -6 to 6
- w_self: bfloat16 [256, 256], P('feat'), may hold values from -0.375 to 0.375
- w_neigh: bfloat16 [256, 256], P('feat'), may hold values from -0.75 to 0.75
- bias: float32 [256], P('feat'), may hold values from -3 to 3
- grad_out: bfloat16 [131072, 256], P('dom', 'feat'), may hold values from -6 to 6
- degree: int32 [131072], P('dom'), may hold values from 1 to 18188, as said below
- tiles: bfloat16 [8192, 128, 128], P('dom'), may hold values from 0 to 1, as said below
- tile_src: int32 [8192], P('dom'), may hold values from 0 to 15
- tile_dst: int32 [8192], P('dom'), may hold values from 0 to 15
- tile_count: int32 [64], P('dom'), may hold values from 32 to 128, as said below
- halo_adj: bfloat16 [131072, 1536], P('dom'), may hold values from 0 to 1, as said below
- send_rows: int32 [64, 64, 24], P('dom'), may hold values from 0 to 2047
- send_count: int32 [64, 64], P('dom'), may hold values from 0 to 24, as said below
- hub_adj: bfloat16 [131072, 256], P('dom'), may hold values from 0 to 1, as said below
- hub_local: int32 [256], P('dom'), may hold values from 0 to 2047
Outputs:
- output: bfloat16 [131072, 256], P('dom', 'feat')
- grad_features: bfloat16 [131072, 256], P('dom', 'feat')
- grad_self: float32 [256, 256], P('feat')
- grad_neigh: float32 [256, 256], P('feat')
- grad_bias: float32 [256], P('feat')
The draws below stay inside these ranges and needn't reach their ends.
Inputs may be any that keep to these rules, and one draw needn't show every extreme that they name: `tiles`: entries are 0 or 1. `halo_adj`: entries are 0 or 1. `hub_adj`: entries are 0 or 1. `tile_count`: some partition uses all 128 slots of its list. `send_count`: A partition sends nothing to itself; every partition fills all 24 slots to some other partition. Each node's degree exceeds its number of edges in tiles, halo_adj and hub_adj by 1 to 11, except one node, whose degree is the maximum.
All inputs are finite; a program needn't handle non-finite values.
Results may differ from the reference program's by a relative error of at most 0.015.
Values may be sent and summed in bfloat16 or wider, within the bound.
No kernel may reach another device: no remote copies, remote signals or barrier semaphores. Data moves between devices by JAX's collectives and lax.ppermute only.
A program may use at most 64 MiB of HBM per device.

```python
import jax
import jax.numpy as jnp
from jax import lax

FIN = 256
FOUT = 256
BLOCK = 128
BLK_DEV = 16
SLOT = 24
HUB_DEV = 4
TILES_DEV = 128
NODES = 131072
HUBS = 256
N_DOM = 64
N_FEAT = 4


def graph_draw(key):
    key = jax.random.fold_in(key, 11)
    keys = jax.random.split(key, 8)
    tile_bits = (jax.random.randint(keys[0], (N_DOM * TILES_DEV, BLOCK, BLOCK), 0, 1000) < 5).astype(jnp.int32)
    targets = jax.random.randint(keys[1], (N_DOM * TILES_DEV,), 0, BLK_DEV).astype(jnp.int32)
    counts = jax.random.randint(keys[2], (N_DOM,), TILES_DEV // 4, TILES_DEV + 1)
    busiest = jax.random.randint(keys[3], (), 0, N_DOM)
    counts = jnp.where(jnp.arange(N_DOM) == busiest, TILES_DEV, counts).astype(jnp.int32)
    halo_bits = (jax.random.randint(keys[4], (NODES, N_DOM * SLOT), 0, 1000) < 4).astype(jnp.int32)
    hub_bits = (jax.random.randint(keys[5], (NODES, HUBS), 0, 100) < 1).astype(jnp.int32)
    extra = jax.random.randint(keys[6], (NODES,), 1, 12).astype(jnp.int32)
    live = (jnp.arange(TILES_DEV, dtype=jnp.int32)[None, :] < counts[:, None]).astype(jnp.int32)
    row_edges = jnp.sum(tile_bits, axis=2).reshape(N_DOM, TILES_DEV, BLOCK) * live[:, :, None]
    onehot = (targets.reshape(N_DOM, TILES_DEV)[:, :, None] == jnp.arange(BLK_DEV, dtype=jnp.int32)[None, None, :]).astype(jnp.int32)
    local_edges = jnp.sum(onehot[:, :, :, None] * row_edges[:, :, None, :], axis=1).reshape(NODES)
    degrees = local_edges + jnp.sum(halo_bits, axis=1) + jnp.sum(hub_bits, axis=1) + extra
    chosen = jax.random.randint(keys[7], (), 0, NODES)
    ceiling = TILES_DEV * BLOCK + N_DOM * SLOT + HUBS + 12
    degrees = jnp.where(jnp.arange(NODES) == chosen, ceiling, degrees)
    return (tile_bits, targets, counts, halo_bits, hub_bits, degrees.astype(jnp.int32))


def draw_tiles(key, part):
    return graph_draw(key)[0].astype(jnp.bfloat16)


def draw_tile_dst(key, part):
    return graph_draw(key)[1]


def draw_tile_count(key, part):
    return graph_draw(key)[2]


def draw_halo_adj(key, part):
    return graph_draw(key)[3].astype(jnp.bfloat16)


def draw_hub_adj(key, part):
    return graph_draw(key)[4].astype(jnp.bfloat16)


def draw_degree(key, part):
    return graph_draw(key)[5]


def draw_send_count(key, part):
    key = jax.random.fold_in(key, 5)
    counts = jax.random.randint(key, (N_DOM, N_DOM), 0, SLOT + 1)
    places = jnp.arange(N_DOM)
    counts = jnp.where(places[:, None] == places[None, :], 0, counts)
    counts = jnp.where(places[None, :] == (places[:, None] + 1) % N_DOM, SLOT, counts)
    return counts.astype(jnp.int32)


def place_ends(entries, key, low, largest):
    longest = entries.shape.index(max(entries.shape))
    spots = []
    for shift in (0, 1):
        where = [jax.random.randint(jax.random.fold_in(key, axis), (), 0, length) for axis, length in enumerate(entries.shape)]
        where[longest] = (where[longest] + shift) % entries.shape[longest]
        spots.append(tuple(where))
    return entries.at[spots[0]].set(low).at[spots[1]].set(largest)


def levels(stream_key, extent, pieces, smallest, top_value):
    level, own = 1.0, jax.random.fold_in(stream_key, 6)
    for axis_at, parts in pieces:
        heights = jnp.exp(jax.random.uniform(jax.random.fold_in(own, axis_at), (parts,), jnp.float32, smallest / len(pieces), top_value / len(pieces)))
        level = level * jnp.repeat(heights, extent[axis_at] // parts).reshape([-1 if axis == axis_at else 1 for axis in range(len(extent))])
    return level


def gaussian(own_key, dims, scale, bound, shards=(), kind=jnp.bfloat16):
    result = scale * jax.random.normal(own_key, dims, jnp.float32)
    if shards:
        result = result * levels(own_key, dims, shards, -0.22, 0.18)
    return jnp.clip(result, -bound, bound).astype(kind)


def setup_inputs(seed: int = 0) -> dict:
    seeds = jax.random.split(jax.random.key(seed), 16)
    return {
        "features": gaussian(seeds[0], (NODES, FIN), 1.0, 6.0, ((0, 64), (1, 4))),
        "w_self": gaussian(seeds[1], (FIN, FOUT), FIN ** -0.5, 0.375, ((0, 4),)),
        "w_neigh": gaussian(seeds[2], (FIN, FOUT), (FIN // 4) ** -0.5, 0.75, ((0, 4),)),
        "bias": gaussian(seeds[3], (FOUT,), 0.5, 3.0, ((0, 4),), jnp.float32),
        "grad_out": gaussian(seeds[4], (NODES, FOUT), 1.0, 6.0, ((0, 64), (1, 4))),
        "degree": draw_degree(jax.random.fold_in(seeds[15], 71), 0),
        "tiles": draw_tiles(jax.random.fold_in(seeds[15], 71), 0),
        "tile_src": place_ends(jax.random.randint(seeds[7], (N_DOM * TILES_DEV,), 0, BLK_DEV), jax.random.fold_in(seeds[7], 1), 0, BLK_DEV - 1).astype(jnp.int32),
        "tile_dst": draw_tile_dst(jax.random.fold_in(seeds[15], 71), 0),
        "tile_count": draw_tile_count(jax.random.fold_in(seeds[15], 71), 0),
        "halo_adj": draw_halo_adj(jax.random.fold_in(seeds[15], 71), 0),
        "send_rows": place_ends(jax.random.randint(seeds[11], (N_DOM, N_DOM, SLOT), 0, BLK_DEV * BLOCK), jax.random.fold_in(seeds[11], 1), 0, (BLK_DEV * BLOCK) - 1).astype(jnp.int32),
        "send_count": draw_send_count(jax.random.fold_in(seeds[15], 71), 0),
        "hub_adj": draw_hub_adj(jax.random.fold_in(seeds[15], 71), 0),
        "hub_local": place_ends(jax.random.randint(seeds[14], (HUBS,), 0, BLK_DEV * BLOCK), jax.random.fold_in(seeds[14], 1), 0, (BLK_DEV * BLOCK) - 1).astype(jnp.int32),
    }


def silu_slope(value):
    sigma = jax.nn.sigmoid(value)
    return sigma * (1.0 + value * (1.0 - sigma))


def reference(features, w_self, w_neigh, bias, grad_out, degree, tiles, tile_src, tile_dst, tile_count, halo_adj, send_rows, send_count, hub_adj, hub_local):
    rows_dev = BLK_DEV * BLOCK
    fin_dev = FIN // N_FEAT
    owners = jnp.arange(N_DOM, dtype=jnp.int32)
    slots = jnp.arange(SLOT, dtype=jnp.int32)
    live_slot = slots[None, None, :] < send_count[:, :, None]
    send_flat = owners[:, None, None] * rows_dev + send_rows
    hub_ids = (jnp.arange(HUBS, dtype=jnp.int32) // HUB_DEV) * rows_dev + hub_local
    hub_rows = features[hub_ids]
    feat_dev = features.reshape(N_DOM, rows_dev, FIN)
    tiles_dev = tiles.reshape(N_DOM, TILES_DEV, BLOCK, BLOCK)
    source_dev = tile_src.reshape(N_DOM, TILES_DEV)
    target_dev = tile_dst.reshape(N_DOM, TILES_DEV)
    live_tile = (jnp.arange(TILES_DEV, dtype=jnp.int32)[None, :] < tile_count[:, None]).astype(jnp.float32)
    halo_dev = halo_adj.reshape(N_DOM, rows_dev, N_DOM * SLOT)
    hubadj_dev = hub_adj.reshape(N_DOM, rows_dev, HUBS)
    degrees = degree.astype(jnp.float32).reshape(N_DOM, rows_dev)

    def aggregate(owner):
        blocks = feat_dev[owner].reshape(BLK_DEV, BLOCK, FIN)
        picked = blocks[source_dev[owner]].astype(jnp.float32)
        products = jnp.einsum("tij,tjf->tif", tiles_dev[owner].astype(jnp.float32), picked)
        products = products * live_tile[owner][:, None, None]
        local_sum = jax.ops.segment_sum(products, target_dev[owner], num_segments=BLK_DEV).reshape(rows_dev, FIN)
        incoming = features[send_flat[:, owner, :]] * live_slot[:, owner, :, None].astype(jnp.bfloat16)
        halo_sum = jnp.dot(halo_dev[owner], incoming.reshape(N_DOM * SLOT, FIN), preferred_element_type=jnp.float32)
        hub_sum = jnp.dot(hubadj_dev[owner], hub_rows, preferred_element_type=jnp.float32)
        return ((local_sum + halo_sum + hub_sum) / degrees[owner][:, None]).astype(jnp.bfloat16)

    mean = lax.map(aggregate, owners).reshape(NODES, FIN)
    pre = jnp.zeros((NODES, FOUT), jnp.float32) + bias[None, :]
    for group in range(N_FEAT):
        low = group * fin_dev
        term = jnp.dot(features[:, low:low + fin_dev], w_self[low:low + fin_dev], preferred_element_type=jnp.float32)
        term = term + jnp.dot(mean[:, low:low + fin_dev], w_neigh[low:low + fin_dev], preferred_element_type=jnp.float32)
        pre = pre + lax.optimization_barrier(term.astype(jnp.bfloat16)).astype(jnp.float32)
    output = jax.nn.silu(pre).astype(jnp.bfloat16)
    grad_pre = (grad_out.astype(jnp.float32) * silu_slope(pre)).astype(jnp.bfloat16)
    grad_self = jnp.dot(features.T, grad_pre, preferred_element_type=jnp.float32)
    grad_neigh = jnp.dot(mean.T, grad_pre, preferred_element_type=jnp.float32)
    grad_bias = jnp.sum(grad_pre.astype(jnp.float32), axis=0)
    grad_input = jnp.dot(grad_pre, w_self.T, preferred_element_type=jnp.float32)
    grad_agg = jnp.dot(grad_pre, w_neigh.T, preferred_element_type=jnp.float32)
    grad_mean = (grad_agg / degrees.reshape(NODES)[:, None]).astype(jnp.bfloat16)
    gmean_dev = grad_mean.reshape(N_DOM, rows_dev, FIN)

    def spread(owner):
        picked = gmean_dev[owner].reshape(BLK_DEV, BLOCK, FIN)[target_dev[owner]].astype(jnp.float32)
        products = jnp.einsum("tji,tjf->tif", tiles_dev[owner].astype(jnp.float32), picked)
        products = products * live_tile[owner][:, None, None]
        local_back = jax.ops.segment_sum(products, source_dev[owner], num_segments=BLK_DEV).reshape(rows_dev, FIN)
        halo_back = jnp.dot(halo_dev[owner].T, gmean_dev[owner], preferred_element_type=jnp.float32).reshape(N_DOM, SLOT, FIN)
        hub_back = jnp.dot(hubadj_dev[owner].T, gmean_dev[owner], preferred_element_type=jnp.float32)
        return local_back, halo_back, hub_back

    local_back, halo_back, hub_back = lax.map(spread, owners)
    back_rows = jnp.transpose(halo_back, (1, 0, 2, 3)) * live_slot[..., None].astype(jnp.float32)
    total = grad_input + local_back.reshape(NODES, FIN)
    total = total.at[send_flat.reshape(-1)].add(back_rows.reshape(-1, FIN))
    total = total.at[hub_ids].add(jnp.sum(hub_back, axis=0))
    return output, total.astype(jnp.bfloat16), grad_self, grad_neigh, grad_bias
```

```python
import functools

import jax
import jax.numpy as jnp
from jax import lax
from jax.experimental import pallas as pl
from jax.experimental.pallas import tpu as pltpu
from jax.sharding import PartitionSpec as P

BF = jnp.bfloat16
F32 = jnp.float32
I32 = jnp.int32

PEERS = 64
FEATS = 4
SLOT = 24
HUBS = 4
ROWS = 16
WIDE = 24
LANES = 128
FIN = 64
FOUT = 256
NODES = 2048
BLOCK = 128
TILES = 128
HALO = PEERS * SLOT
HUB_ALL = PEERS * HUBS
WPACK = 144

VMEM_LIMIT = 48 * 1024 * 1024


def matmul(left, right):
    return lax.dot_general(
        left, right, (((1,), (0,)), ((), ())), preferred_element_type=F32
    )


def matmul_nt(left, right):
    return lax.dot_general(
        left, right, (((1,), (1,)), ((), ())), preferred_element_type=F32
    )


def params(semantics=None):
    return pltpu.CompilerParams(
        dimension_semantics=semantics, vmem_limit_bytes=VMEM_LIMIT
    )


def cost(flops, moved):
    return pl.CostEstimate(flops=flops, bytes_accessed=moved, transcendentals=0)


def iota(shape, axis):
    return lax.broadcasted_iota(I32, shape, axis)


def pick_hubs():
    hub = iota((HUB_ALL, PEERS * 8), 0)
    place = iota((HUB_ALL, PEERS * 8), 1)
    same = (hub // HUBS == place // 8) & (hub % HUBS == place % 8)
    return same.astype(F32).astype(BF)


def gather_kernel(hub_ref, send_ref, count_ref, feat_ref, wire_ref, index_ref):
    slot = iota((SLOT, PEERS), 0)
    sent = jnp.where(slot < count_ref[...], send_ref[...], -1)
    place = iota((8, PEERS), 0)
    hubs = jnp.full((8, PEERS), -1, I32)
    for h in range(HUBS):
        hubs = jnp.where(place == h, hub_ref[h], hubs)
    rows = jnp.concatenate([sent, hubs], axis=0)
    high = lax.shift_right_arithmetic(rows, 6)
    low = rows - high * 64
    split = jnp.concatenate([high, low], axis=0).astype(F32).astype(BF)
    count = PEERS * ROWS
    spread = (iota((PEERS, count), 0) == iota((PEERS, count), 1) // ROWS)
    wide = matmul(split, spread.astype(F32).astype(BF))
    wide = wide[:32] * 64.0 + wide[32:]
    mine = iota((ROWS, count), 0) == iota((ROWS, count), 1) % ROWS
    left = jnp.sum(jnp.where(mine, wide[:ROWS], 0.0), axis=0, keepdims=True)
    right = jnp.sum(jnp.where(mine, wide[ROWS:], 0.0), axis=0, keepdims=True)
    both = jnp.concatenate([left, right], axis=1)
    index_ref[...] = jnp.broadcast_to(both, (8, 2 * count))
    target = both.astype(I32)
    step = 256
    total = jnp.zeros((FIN, 2 * count), F32)
    node = iota((step, 2 * count), 0)
    for k in range(NODES // step):
        hot = (node == target - k * step).astype(F32).astype(BF)
        total += matmul(feat_ref[:, k * step:(k + 1) * step], hot)
    stacked = jnp.concatenate([total[:, :count], total[:, count:]], axis=0)
    wire_ref[...] = stacked.T.astype(BF)


def gather_rows(hub_local, send, count, feat):
    slots = PEERS * ROWS
    full = lambda *_: (0, 0)
    return pl.pallas_call(
        gather_kernel,
        grid_spec=pltpu.PrefetchScalarGridSpec(
            num_scalar_prefetch=1,
            grid=(1,),
            in_specs=[
                pl.BlockSpec((SLOT, PEERS), full),
                pl.BlockSpec((1, PEERS), full),
                pl.BlockSpec((FIN, NODES), full),
            ],
            out_specs=[
                pl.BlockSpec((slots, LANES), full),
                pl.BlockSpec((8, 2 * slots), full),
            ],
        ),
        out_shape=[
            jax.ShapeDtypeStruct((slots, LANES), BF),
            jax.ShapeDtypeStruct((8, 2 * slots), F32),
        ],
        compiler_params=params(),
        cost_estimate=cost(2 * 2 * slots * NODES * 256, 1000000),
        name="gather_rows",
    )(hub_local, send, count, feat)


def local_kernel(src_ref, dst_ref, count_ref, tiles_ref, feat_ref, sum_ref, adj_ref):
    step = pl.program_id(0)
    group = tiles_ref.shape[0]

    @pl.when(step == 0)
    def clear():
        adj_ref[...] = jnp.zeros_like(adj_ref)

    for j in range(group):
        t = step * group + j

        @pl.when(t < count_ref[0])
        def add():
            rows = pl.ds(pl.multiple_of(dst_ref[t] * BLOCK, BLOCK), BLOCK)
            cols = pl.ds(pl.multiple_of(src_ref[t] * BLOCK, BLOCK), BLOCK)
            adj_ref[rows, cols] += tiles_ref[j]

    @pl.when(step == pl.num_programs(0) - 1)
    def finish():
        width = 256
        for k in range(NODES // width):
            part = adj_ref[k * width:(k + 1) * width, :]
            sum_ref[:, k * width:(k + 1) * width] = matmul_nt(feat_ref[...], part)


def local_sum(src, dst, count, tiles, feat):
    group = 16
    return pl.pallas_call(
        local_kernel,
        grid_spec=pltpu.PrefetchScalarGridSpec(
            num_scalar_prefetch=3,
            grid=(TILES // group,),
            in_specs=[
                pl.BlockSpec((group, BLOCK, BLOCK), lambda i, *_: (i, 0, 0)),
                pl.BlockSpec((FIN, NODES), lambda i, *_: (0, 0)),
            ],
            out_specs=[
                pl.BlockSpec((FIN, NODES), lambda i, *_: (0, 0)),
                pl.BlockSpec((NODES, NODES), lambda i, *_: (0, 0)),
            ],
        ),
        out_shape=[
            jax.ShapeDtypeStruct((FIN, NODES), F32),
            jax.ShapeDtypeStruct((NODES, NODES), BF),
        ],
        compiler_params=params(("arbitrary",)),
        cost_estimate=cost(2 * NODES * NODES * 256, 13000000),
        name="local_sum",
    )(src, dst, count, tiles, feat)


def mean_kernel(wire_ref, halo_ref, hub_ref, local_ref, degree_ref, mean_ref, rows_ref, hubs_ref):
    @pl.when(pl.program_id(0) == 0)
    def unpack():
        wire = wire_ref[...].astype(F32).reshape(PEERS, ROWS, LANES)
        left = wire[:, :, :FIN]
        right = wire[:, :, FIN:]
        rows = jnp.concatenate([left, right[:, :8]], axis=1)
        rows_ref[...] = rows.reshape(HALO, FIN).astype(BF)
        owned = right[:, 8:].reshape(PEERS * 8, FIN).astype(BF)
        hubs_ref[...] = matmul(pick_hubs(), owned).astype(BF)

    total = matmul(halo_ref[...], rows_ref[...]) + matmul(hub_ref[...], hubs_ref[...])
    total = total.T + local_ref[...]
    mean_ref[...] = (total / degree_ref[...].astype(F32)).astype(BF)


def mean_rows(wire, halo_adj, hub_adj, local, degree):
    chunk = 512
    return pl.pallas_call(
        mean_kernel,
        grid=(NODES // chunk,),
        in_specs=[
            pl.BlockSpec((PEERS * ROWS, LANES), lambda i: (0, 0)),
            pl.BlockSpec((chunk, HALO), lambda i: (i, 0)),
            pl.BlockSpec((chunk, HUB_ALL), lambda i: (i, 0)),
            pl.BlockSpec((FIN, chunk), lambda i: (0, i)),
            pl.BlockSpec((1, chunk), lambda i: (0, i)),
        ],
        out_specs=pl.BlockSpec((FIN, chunk), lambda i: (0, i)),
        out_shape=jax.ShapeDtypeStruct((FIN, NODES), BF),
        scratch_shapes=[
            pltpu.VMEM((HALO, FIN), BF),
            pltpu.VMEM((HUB_ALL, FIN), BF),
        ],
        compiler_params=params(("arbitrary",)),
        cost_estimate=cost(2 * NODES * (HALO + HUB_ALL) * 256, 8000000),
        name="mean_rows",
    )(wire, halo_adj, hub_adj, local, degree)


def dense_kernel(
    mine_ref, feat_ref, gout_ref, mean0_ref, mean1_ref, mean2_ref, mean3_ref,
    pack_ref, degree_ref, halo_ref, hub_ref,
    out_ref, gmean_ref, ginput_ref, wire_ref,
    weight_ref, bias_ref, back_ref, pre_ref, halo_acc, hub_acc, grad_acc,
):
    step = pl.program_id(0)
    mine = mine_ref[0]
    own = pl.multiple_of(mine * FIN, FIN)
    means = (mean0_ref, mean1_ref, mean2_ref, mean3_ref)

    @pl.when(step == 0)
    def prepare():
        eye = iota((FIN, FIN), 0) == iota((FIN, FIN), 1)
        for g in range(FEATS):
            both = pack_ref[g, :2 * FIN, :].astype(F32)
            weight_ref[g] = both.T.astype(BF)
            parts = pack_ref[g, 2 * FIN:2 * FIN + 16, :].astype(F32)
            row = parts[0:1, :FIN] + parts[1:2, :FIN] + parts[2:3, :FIN]
            column = jnp.sum(jnp.where(eye, row, 0.0), axis=1, keepdims=True)
            bias_ref[g * FIN:(g + 1) * FIN, :] = jnp.broadcast_to(column, (FIN, LANES))
        back_ref[...] = pack_ref[mine, :2 * FIN, :]
        halo_acc[...] = jnp.zeros_like(halo_acc)
        hub_acc[...] = jnp.zeros_like(hub_acc)
        grad_acc[...] = jnp.zeros_like(grad_acc)

    chunk = feat_ref.shape[1]
    pre = jnp.tile(bias_ref[...], (1, chunk // LANES))
    for k in range(FEATS):
        g = lax.rem(mine - k + FEATS, FEATS)
        rows = pl.ds(pl.multiple_of(g * FIN, FIN), FIN)
        both = jnp.concatenate([feat_ref[rows, :], means[k][...]], axis=0)
        pre = pre + matmul(weight_ref[g], both).astype(BF).astype(F32)
    sigma = 1.0 / (1.0 + jnp.exp(-pre))
    pre_ref[...] = pre * sigma
    out_ref[...] = pre_ref[pl.ds(own, FIN), :].astype(BF)
    slope = sigma * (1.0 + pre * (1.0 - sigma))
    gpre = (gout_ref[...].astype(F32) * slope).astype(BF)
    back = matmul(back_ref[...], gpre)
    ginput_ref[...] = back[:FIN]
    gmean = (back[FIN:] / degree_ref[...].astype(F32)).astype(BF)
    gmean_ref[...] = gmean
    left = jnp.concatenate(
        [feat_ref[pl.ds(own, FIN), :], mean0_ref[...], jnp.ones((16, chunk), BF)], axis=0
    )
    grad_acc[...] += matmul_nt(left, gpre)
    halo_acc[...] += matmul(gmean, halo_ref[...])
    hub_acc[...] += matmul(gmean, hub_ref[...])

    @pl.when(step == pl.num_programs(0) - 1)
    def ship():
        rows = halo_acc[...].T.reshape(PEERS, SLOT, FIN)
        hubs = matmul(hub_acc[...].astype(BF), pick_hubs()).T.reshape(PEERS, 8, FIN)
        bias = grad_acc[2 * FIN:2 * FIN + 1, :]
        row = bias[:, :FIN]
        for g in range(1, FEATS):
            row = jnp.where(mine == g, bias[:, g * FIN:(g + 1) * FIN], row)
        high = row.astype(BF).astype(F32)
        place = iota((8, FIN), 0)
        extra = jnp.where(place == 4, high, jnp.where(place == 5, row - high, 0.0))
        hubs = hubs + extra[None]
        right = jnp.concatenate([rows[:, 16:], hubs], axis=1)
        main = jnp.concatenate([rows[:, :16], right], axis=2)
        grads = grad_acc[:2 * FIN, :].reshape(16, 8, FOUT)
        grads = jnp.stack([grads[:, :, :LANES], grads[:, :, LANES:]], axis=1)
        grads = grads.reshape(32, 8, LANES)
        high = grads.astype(BF).astype(F32)
        low = grads - high
        swap = lambda x: jnp.concatenate([x[:, 4:], x[:, :4]], axis=1)
        first = iota((32, 8, LANES), 1) < 4
        even = jnp.where(first, high, swap(low))
        odd = jnp.where(first, swap(high), low)
        pieces = jnp.stack([even, odd], axis=1).reshape(PEERS, 8, LANES)
        wire = jnp.concatenate([main, pieces], axis=1)
        wire_ref[...] = wire.reshape(PEERS * WIDE, LANES).astype(BF)


def dense(mine, feat, gout, means, pack, degree, halo_adj, hub_adj):
    chunk = 256
    full = lambda i, *_: (0, 0)
    column = lambda i, *_: (0, i)
    return pl.pallas_call(
        dense_kernel,
        grid_spec=pltpu.PrefetchScalarGridSpec(
            num_scalar_prefetch=1,
            grid=(NODES // chunk,),
            in_specs=[
                pl.BlockSpec((FEATS * FIN, chunk), column),
                pl.BlockSpec((FOUT, chunk), column),
            ]
            + [pl.BlockSpec((FIN, chunk), column)] * FEATS
            + [
                pl.BlockSpec((FEATS, WPACK, FOUT), lambda i, *_: (0, 0, 0)),
                pl.BlockSpec((1, chunk), column),
                pl.BlockSpec((chunk, HALO), lambda i, *_: (i, 0)),
                pl.BlockSpec((chunk, HUB_ALL), lambda i, *_: (i, 0)),
            ],
            out_specs=[
                pl.BlockSpec((FIN, chunk), column),
                pl.BlockSpec((FIN, chunk), column),
                pl.BlockSpec((FIN, chunk), column),
                pl.BlockSpec((PEERS * WIDE, LANES), full),
            ],
            scratch_shapes=[
                pltpu.VMEM((FEATS, FOUT, 2 * FIN), BF),
                pltpu.VMEM((FOUT, LANES), F32),
                pltpu.VMEM((2 * FIN, FOUT), BF),
                pltpu.VMEM((FOUT, chunk), F32),
                pltpu.VMEM((FIN, HALO), F32),
                pltpu.VMEM((FIN, HUB_ALL), F32),
                pltpu.VMEM((2 * FIN + 16, FOUT), F32),
            ],
        ),
        out_shape=[
            jax.ShapeDtypeStruct((FIN, NODES), BF),
            jax.ShapeDtypeStruct((FIN, NODES), BF),
            jax.ShapeDtypeStruct((FIN, NODES), F32),
            jax.ShapeDtypeStruct((PEERS * WIDE, LANES), BF),
        ],
        compiler_params=params(("arbitrary",)),
        cost_estimate=cost(2 * NODES * 2048 * 256, 12000000),
        name="dense",
    )(mine, feat, gout, *means, pack, degree, halo_adj, hub_adj)


def back_kernel(ginput_ref, gmean_ref, adj_ref, total_ref):
    total_ref[...] = ginput_ref[...] + matmul(gmean_ref[...], adj_ref[...])


def local_back(ginput, gmean, adj):
    chunk = 512
    return pl.pallas_call(
        back_kernel,
        grid=(NODES // chunk,),
        in_specs=[
            pl.BlockSpec((FIN, chunk), lambda i: (0, i)),
            pl.BlockSpec((FIN, NODES), lambda i: (0, 0)),
            pl.BlockSpec((NODES, chunk), lambda i: (0, i)),
        ],
        out_specs=pl.BlockSpec((FIN, chunk), lambda i: (0, i)),
        out_shape=jax.ShapeDtypeStruct((FIN, NODES), F32),
        compiler_params=params(("arbitrary",)),
        cost_estimate=cost(2 * NODES * NODES * 256, 10000000),
        name="local_back",
    )(ginput, gmean, adj)


def reduce_kernel(wire_ref, sums_ref, bias_ref):
    wire = wire_ref[...].astype(F32).reshape(PEERS, WIDE, LANES)
    pieces = jnp.sum(wire[:, 16:], axis=0)
    half = pieces[:4] + pieces[4:]
    both = jnp.concatenate([half, half], axis=0)
    sums_ref[...] = jnp.broadcast_to(both[None], (PEERS // 2, 8, LANES)).reshape(
        PEERS * 4, LANES
    )
    tail = jnp.sum(wire[:, 8:16], axis=0)
    bias_ref[...] = tail[4:5, FIN:] + tail[5:6, FIN:]


def reduce_grads(wire):
    return pl.pallas_call(
        reduce_kernel,
        out_shape=[
            jax.ShapeDtypeStruct((PEERS * 4, LANES), F32),
            jax.ShapeDtypeStruct((1, FIN), F32),
        ],
        compiler_params=params(),
        cost_estimate=cost(1000000, 1000000),
        name="reduce_grads",
    )(wire)


def scatter_kernel(wire_ref, index_ref, total_ref, out_ref, back_ref):
    count = PEERS * ROWS

    @pl.when(pl.program_id(0) == 0)
    def unpack():
        wire = wire_ref[...].astype(F32).reshape(PEERS, WIDE, LANES)
        both = wire[:, :16].reshape(count, LANES).T
        back_ref[...] = jnp.concatenate([both[:FIN], both[FIN:]], axis=1).astype(BF)

    step = out_ref.shape[1]
    target = index_ref[0:1, :].astype(I32) - pl.program_id(0) * step
    hot = (iota((step, 2 * count), 0) == target).astype(F32).astype(BF)
    out_ref[...] = (total_ref[...] + matmul_nt(back_ref[...], hot)).astype(BF)


def scatter_rows(wire, index, total):
    chunk = 256
    count = PEERS * ROWS
    return pl.pallas_call(
        scatter_kernel,
        grid=(NODES // chunk,),
        in_specs=[
            pl.BlockSpec((PEERS * WIDE, LANES), lambda i: (0, 0)),
            pl.BlockSpec((8, 2 * count), lambda i: (0, 0)),
            pl.BlockSpec((FIN, chunk), lambda i: (0, i)),
        ],
        out_specs=pl.BlockSpec((FIN, chunk), lambda i: (0, i)),
        out_shape=jax.ShapeDtypeStruct((FIN, NODES), BF),
        scratch_shapes=[pltpu.VMEM((FIN, 2 * count), BF)],
        compiler_params=params(("arbitrary",)),
        cost_estimate=cost(2 * 2 * count * NODES * 256, 2000000),
        name="scatter_rows",
    )(wire, index, total)


def three_parts(value):
    high = lax.reduce_precision(value, 8, 7)
    middle = lax.reduce_precision(value - high, 8, 7)
    low = value - high - middle
    return jnp.stack([high, middle, low]).astype(BF)


def on_device(
    features,
    w_self,
    w_neigh,
    bias,
    grad_out,
    degree,
    tiles,
    tile_src,
    tile_dst,
    tile_count,
    halo_adj,
    send_rows,
    send_count,
    hub_adj,
    hub_local,
):
    feat = features.T
    gout = grad_out.T
    mine = lax.axis_index("feat").astype(I32).reshape(1)
    degree = degree.reshape(1, NODES)
    biases = jnp.pad(three_parts(bias), ((0, WPACK - 2 * FIN - 3), (0, FOUT - FIN)))
    pack = jnp.concatenate([w_self, w_neigh, biases], axis=0)
    feat_all = lax.all_gather(feat, "feat", axis=0, tiled=True)
    gout_all = lax.all_gather(gout, "feat", axis=0, tiled=True)
    pack_all = lax.all_gather(pack, "feat", axis=0, tiled=True)
    pack_all = pack_all.reshape(FEATS, WPACK, FOUT)
    send = jnp.transpose(send_rows[0])
    wire, index = gather_rows(hub_local, send, send_count, feat)
    arrived = lax.all_to_all(wire, "dom", split_axis=0, concat_axis=0, tiled=True)
    local, adj = local_sum(tile_src, tile_dst, tile_count, tiles, feat)
    mean = mean_rows(arrived, halo_adj, hub_adj, local, degree)
    means = [mean] + [
        lax.ppermute(mean, "feat", [(j, (j + k) % FEATS) for j in range(FEATS)])
        for k in range(1, FEATS)
    ]
    out, gmean, ginput, wire = dense(
        mine, feat_all, gout_all, means, pack_all, degree, halo_adj, hub_adj
    )
    returned = lax.all_to_all(wire, "dom", split_axis=0, concat_axis=0, tiled=True)
    total = local_back(ginput, gmean, adj)
    sums, grad_bias = reduce_grads(returned)
    shared = lax.all_to_all(sums, "dom", split_axis=0, concat_axis=0, tiled=True)
    grad_features = scatter_rows(returned, index, total)
    grads = shared.reshape(16, 2, 8, LANES).transpose(0, 2, 1, 3).reshape(2 * FIN, FOUT)
    return (
        out.T,
        grad_features.T,
        grads[:FIN],
        grads[FIN:],
        grad_bias.reshape(FIN),
    )


def solution(mesh):
    in_specs = (
        P("dom", "feat"),
        P("feat", None),
        P("feat", None),
        P("feat"),
        P("dom", "feat"),
        P("dom"),
        P("dom", None, None),
        P("dom"),
        P("dom"),
        P("dom"),
        P("dom", None),
        P("dom", None, None),
        P("dom", None),
        P("dom", None),
        P("dom"),
    )
    out_specs = (P("dom", "feat"), P("dom", "feat"), P("feat", None), P("feat", None), P("feat"))
    return jax.shard_map(
        on_device, mesh=mesh, in_specs=in_specs, out_specs=out_specs, check_vma=False
    )
```

```python
import jax
import jax.numpy as jnp
from jax import lax
from jax.experimental import pallas as pl
from jax.experimental.pallas import tpu as pltpu
from jax.sharding import PartitionSpec as P

BF = jnp.bfloat16
F32 = jnp.float32
I32 = jnp.int32

PEERS = 64
FEATS = 4
SLOT = 24
HUBS = 4
ROWS = 16
WIDE = 24
LANES = 128
FIN = 64
FOUT = 256
NODES = 2048
BLOCK = 128
TILES = 128
HALO = PEERS * SLOT
HUB_ALL = PEERS * HUBS
BUNDLE = 160
PACK = 2 * FIN
HALF = NODES // 2
SLOTS = PEERS * ROWS
CHUNK = 256

def matmul(left, right):
    return lax.dot_general(
        left, right, (((1,), (0,)), ((), ())), preferred_element_type=F32
    )


def matmul_nt(left, right):
    return lax.dot_general(
        left, right, (((1,), (1,)), ((), ())), preferred_element_type=F32
    )


def params(mebibytes=24):
    return pltpu.CompilerParams(vmem_limit_bytes=mebibytes * 1024 * 1024)


def cost(flops, moved):
    return pl.CostEstimate(flops=flops, bytes_accessed=moved, transcendentals=0)


def in_vmem(count):
    return [pl.BlockSpec(memory_space=pltpu.VMEM)] * count


def in_hbm(count):
    return [pl.BlockSpec(memory_space=pltpu.HBM)] * count


def keep_hbm(*values):
    return [pltpu.with_memory_space_constraint(value, pltpu.HBM) for value in values]


def iota(shape, axis):
    return lax.broadcasted_iota(I32, shape, axis)


def pick_hubs():
    hub = iota((HUB_ALL, PEERS * 8), 0)
    place = iota((HUB_ALL, PEERS * 8), 1)
    same = (hub // HUBS == place // 8) & (hub % HUBS == place % 8)
    return same.astype(F32).astype(BF)


def start_all(pairs, sems):
    copies = [
        pltpu.make_async_copy(src, dst, sems.at[i]) for i, (src, dst) in enumerate(pairs)
    ]
    for copy in copies:
        copy.start()
    return copies


def slot_targets(hub_ref, send_ref, count_ref):
    slot = iota((SLOT, PEERS), 0)
    sent = jnp.where(slot < count_ref[...], send_ref[...], -1)
    place = iota((8, PEERS), 0)
    hubs = jnp.full((8, PEERS), -1, I32)
    for h in range(HUBS):
        hubs = jnp.where(place == h, hub_ref[h], hubs)
    rows = jnp.concatenate([sent, hubs], axis=0)
    high = lax.shift_right_arithmetic(rows, 6)
    low = rows - high * 64
    split = jnp.concatenate([high, low], axis=0).astype(F32).astype(BF)
    spread = (iota((PEERS, SLOTS), 0) == iota((PEERS, SLOTS), 1) // ROWS)
    wide = matmul(split, spread.astype(F32).astype(BF))
    wide = wide[:32] * 64.0 + wide[32:]
    mine = iota((ROWS, SLOTS), 0) == iota((ROWS, SLOTS), 1) % ROWS
    left = jnp.sum(jnp.where(mine, wide[:ROWS], 0.0), axis=0, keepdims=True)
    right = jnp.sum(jnp.where(mine, wide[ROWS:], 0.0), axis=0, keepdims=True)
    return jnp.concatenate([left, right], axis=1)


def front_kernel(
    hub_hbm, send_hbm, count_hbm, feat_hbm, gout_hbm, self_hbm, neigh_hbm, bias_hbm, degree_hbm,
    wire_ref, index_ref, bundle_hbm,
    hub_ref, send_ref, count_ref, self_ref, neigh_ref, bias_ref, degree_ref, bundle_ref, sems,
    out_sem,
):
    pairs = [
        (hub_hbm, hub_ref),
        (send_hbm, send_ref),
        (count_hbm, count_ref),
        (feat_hbm, bundle_ref.at[pl.ds(0, FIN)]),
        (self_hbm, self_ref),
        (neigh_hbm, neigh_ref),
        (bias_hbm, bias_ref),
        (degree_hbm, degree_ref),
        (gout_hbm, bundle_ref.at[pl.ds(FIN, FIN)]),
    ]
    copies = start_all(pairs, sems)
    for copy in copies[:3]:
        copy.wait()
    both = slot_targets(hub_ref, send_ref, count_ref)
    index_ref[:8] = jnp.broadcast_to(both, (8, 2 * SLOTS))
    for copy in copies[4:8]:
        copy.wait()
    index_ref[8:] = jnp.broadcast_to(degree_ref[...].astype(F32), (8, NODES))
    for i in range(4):
        rows = slice(16 * i, 16 * i + 16)
        bundle_ref[PACK:PACK + 16, FOUT * i:FOUT * (i + 1)] = self_ref[rows]
        bundle_ref[PACK:PACK + 16, FOUT * (i + 4):FOUT * (i + 5)] = neigh_ref[rows]
    bias = bias_ref[...]
    high = bias.astype(BF).astype(F32)
    middle = (bias - high).astype(BF).astype(F32)
    low = bias - high - middle
    place = iota((16, FIN), 0)
    parts = jnp.where(
        place == 0, high, jnp.where(place == 1, middle, jnp.where(place == 2, low, 0.0))
    )
    parts = jnp.concatenate([parts, jnp.zeros((16, LANES - FIN), F32)], axis=1).astype(BF)
    bundle_ref[PACK + 16:] = jnp.zeros((16, NODES), BF)
    bundle_ref[PACK + 16:, :LANES] = parts
    copies[3].wait()
    copies[8].wait()
    (outgoing,) = start_all([(bundle_ref, bundle_hbm)], out_sem)
    target = both.astype(I32)
    step = 256
    total = jnp.zeros((FIN, 2 * SLOTS), F32)
    node = iota((step, 2 * SLOTS), 0)
    for k in range(NODES // step):
        hot = (node == target - k * step).astype(F32).astype(BF)
        total += matmul(bundle_ref[:FIN, k * step:(k + 1) * step], hot)
    stacked = jnp.concatenate([total[:, :SLOTS], total[:, SLOTS:]], axis=0)
    wire_ref[...] = stacked.T.astype(BF)
    outgoing.wait()


def front(*operands):
    return pl.pallas_call(
        front_kernel,
        in_specs=in_hbm(9),
        out_specs=in_vmem(2) + in_hbm(1),
        out_shape=[
            jax.ShapeDtypeStruct((SLOTS, LANES), BF),
            pltpu.VMEM((16, NODES), F32),
            pltpu.HBM((BUNDLE, NODES), BF),
        ],
        scratch_shapes=[
            pltpu.SMEM((HUBS,), I32),
            pltpu.VMEM((SLOT, PEERS), I32),
            pltpu.VMEM((1, PEERS), I32),
            pltpu.VMEM((FIN, FOUT), BF),
            pltpu.VMEM((FIN, FOUT), BF),
            pltpu.VMEM((1, FIN), F32),
            pltpu.VMEM((1, NODES), I32),
            pltpu.VMEM((BUNDLE, NODES), BF),
            pltpu.SemaphoreType.DMA((9,)),
            pltpu.SemaphoreType.DMA((1,)),
        ],
        compiler_params=params(),
        cost_estimate=cost(2 * 2 * SLOTS * NODES * 256, 1000000),
        name="front",
    )(*keep_hbm(*operands))


def local_kernel(
    count_ref, src_hbm, dst_hbm, tiles_hbm, bundle_hbm, sum_ref, adj_hbm,
    src_ref, dst_ref, feat_ref, tiles_ref, adj_ref, sems, tile_sems, out_sems,
):
    small = start_all(
        [(src_hbm, src_ref), (dst_hbm, dst_ref), (bundle_hbm.at[pl.ds(0, FIN)], feat_ref)], sems
    )
    groups = tile_sems.shape[0]
    group = TILES // groups
    here = [pl.ds(g * group, group) for g in range(groups)]
    incoming = start_all([(tiles_hbm.at[g], tiles_ref.at[g]) for g in here], tile_sems)
    adj_ref[...] = jnp.zeros_like(adj_ref)
    for copy in small:
        copy.wait()
    for g in range(groups):
        incoming[g].wait()
        for j in range(group):
            t = g * group + j

            @pl.when(t < count_ref[0])
            def add():
                rows = pl.ds(pl.multiple_of(dst_ref[t] * BLOCK, BLOCK), BLOCK)
                cols = pl.ds(pl.multiple_of(src_ref[t] * BLOCK, BLOCK), BLOCK)
                adj_ref[rows, cols] += tiles_ref[t]

    width = 256
    here = [pl.ds(k * width, width) for k in range(NODES // width)]
    outgoing = start_all([(adj_ref.at[k], adj_hbm.at[k]) for k in here], out_sems)
    for k in range(NODES // width):
        part = adj_ref[k * width:(k + 1) * width, :]
        sum_ref[:, k * width:(k + 1) * width] = matmul_nt(feat_ref[...], part)
    for copy in outgoing:
        copy.wait()


def local_sum(src, dst, count, tiles, packed):
    return pl.pallas_call(
        local_kernel,
        in_specs=[pl.BlockSpec(memory_space=pltpu.SMEM)] + in_hbm(4),
        out_specs=in_vmem(1) + in_hbm(1),
        out_shape=[
            pltpu.VMEM((FIN, NODES), F32),
            pltpu.HBM((NODES, NODES), BF),
        ],
        scratch_shapes=[
            pltpu.SMEM((TILES,), I32),
            pltpu.SMEM((TILES,), I32),
            pltpu.VMEM((FIN, NODES), BF),
            pltpu.VMEM((TILES, BLOCK, BLOCK), BF),
            pltpu.VMEM((NODES, NODES), BF),
            pltpu.SemaphoreType.DMA((3,)),
            pltpu.SemaphoreType.DMA((8,)),
            pltpu.SemaphoreType.DMA((8,)),
        ],
        compiler_params=params(),
        cost_estimate=cost(2 * NODES * NODES * 256, 13000000),
        name="local_sum",
    )(count, *keep_hbm(src, dst, tiles, packed))


def adjacency_copies(part, pieces, halo_hbm, hub_hbm, halo_ref, hub_ref, sems):
    piece = HALF // pieces
    pairs = []
    for i in range(pieces):
        there = pl.ds(part * HALF + i * piece, piece)
        pairs.append((halo_hbm.at[there], halo_ref.at[pl.ds(i * piece, piece)]))
    pairs.append((hub_hbm.at[pl.ds(part * HALF, HALF)], hub_ref))
    return start_all(pairs, sems)


def mean_half(part, rows, hubs, halo_ref, hub_ref, local_ref, index_ref, mean_ref, ready):
    chunk = 512
    for i in range(HALF // chunk):
        ready(i)
        here = slice(i * chunk, (i + 1) * chunk)
        whole = slice(part * HALF + i * chunk, part * HALF + (i + 1) * chunk)
        total = matmul(halo_ref[here], rows) + matmul(hub_ref[here], hubs)
        total = total.T + local_ref[:, whole]
        mean_ref[:, here] = (total / index_ref[8:9, whole]).astype(BF)


def first_mean_kernel(
    wire_ref, local_ref, index_ref, halo_hbm, hub_hbm,
    mean_ref, rows_ref, hubs_ref, later_halo, later_hub,
    halo_ref, hub_ref, sems, later_sems,
):
    copies = adjacency_copies(0, 2, halo_hbm, hub_hbm, halo_ref, hub_ref, sems)
    later = []
    wire = wire_ref[...].astype(F32).reshape(PEERS, ROWS, LANES)
    left = wire[:, :, :FIN]
    right = wire[:, :, FIN:]
    rows = jnp.concatenate([left, right[:, :8]], axis=1)
    rows_ref[...] = rows.reshape(HALO, FIN).astype(BF)
    owned = right[:, 8:].reshape(PEERS * 8, FIN).astype(BF)
    hubs_ref[...] = matmul(pick_hubs(), owned).astype(BF)
    copies[-1].wait()

    def ready(i):
        copies[i].wait()
        if i:
            later.extend(
                adjacency_copies(1, 2, halo_hbm, hub_hbm, later_halo, later_hub, later_sems)
            )

    mean_half(
        0, rows_ref[...], hubs_ref[...], halo_ref, hub_ref, local_ref, index_ref, mean_ref, ready
    )
    for copy in later:
        copy.wait()


def later_mean_kernel(rows_ref, hubs_ref, halo_ref, hub_ref, local_ref, index_ref, mean_ref):
    mean_half(
        1, rows_ref[...], hubs_ref[...], halo_ref, hub_ref, local_ref, index_ref, mean_ref,
        lambda i: None,
    )


def first_mean(wire, halo_adj, hub_adj, local, index):
    shapes = [(FIN, HALF), (HALO, FIN), (HUB_ALL, FIN), (HALF, HALO), (HALF, HUB_ALL)]
    return pl.pallas_call(
        first_mean_kernel,
        in_specs=in_vmem(3) + in_hbm(2),
        out_specs=in_vmem(len(shapes)),
        out_shape=[pltpu.VMEM(shape, BF) for shape in shapes],
        scratch_shapes=[
            pltpu.VMEM((HALF, HALO), BF),
            pltpu.VMEM((HALF, HUB_ALL), BF),
            pltpu.SemaphoreType.DMA((3,)),
            pltpu.SemaphoreType.DMA((3,)),
        ],
        compiler_params=params(),
        cost_estimate=cost(HALF * (HALO + HUB_ALL) * 512, 1000000),
        name="mean_rows",
    )(wire, local, index, *keep_hbm(halo_adj, hub_adj))


def later_mean(known, local, index):
    return pl.pallas_call(
        later_mean_kernel,
        in_specs=in_vmem(6),
        out_specs=in_vmem(1)[0],
        out_shape=pltpu.VMEM((FIN, HALF), BF),
        compiler_params=params(),
        cost_estimate=cost(HALF * (HALO + HUB_ALL) * 512, 1000000),
        name="mean_rows",
    )(*known, local, index)


def prepare_weights(mine, packs, weight_ref, bias_ref, back_ref):
    eye = iota((FIN, FIN), 0) == iota((FIN, FIN), 1)
    for k in range(FEATS):
        pieces = [
            packs[k, :16, FOUT * i:FOUT * (i + 1)].astype(F32) for i in range(8)
        ]
        turned = jnp.concatenate(pieces, axis=0).T.astype(BF)
        for b in range(FEATS):
            place = lax.rem(b - mine + FEATS, FEATS)
            rows = pl.ds(pl.multiple_of(place * FIN, FIN), FIN)
            weight_ref[k, rows, :] = turned[b * FIN:(b + 1) * FIN]
        parts = packs[k, 16:, :LANES].astype(F32)
        row = parts[0:1, :FIN] + parts[1:2, :FIN] + parts[2:3, :FIN]
        column = jnp.sum(jnp.where(eye, row, 0.0), axis=1, keepdims=True)
        bias_ref[k * FIN:(k + 1) * FIN, :] = jnp.broadcast_to(column, (FIN, LANES))
    back_ref[...] = weight_ref[0].astype(F32).T.astype(BF)


def ship_gradients(mine, halo_acc, hub_acc, grad_acc, wire_ref):
    rows = halo_acc[...].T.reshape(PEERS, SLOT, FIN)
    hubs = matmul(hub_acc[...].astype(BF), pick_hubs()).T.reshape(PEERS, 8, FIN)
    row = grad_acc[2 * FIN:2 * FIN + 1, :FIN]
    high = row.astype(BF).astype(F32)
    place = iota((8, FIN), 0)
    extra = jnp.where(place == 4, high, jnp.where(place == 5, row - high, 0.0))
    hubs = hubs + extra[None]
    right = jnp.concatenate([rows[:, 16:], hubs], axis=1)
    main = jnp.concatenate([rows[:, :16], right], axis=2)
    grads = pltpu.roll(grad_acc[:2 * FIN, :], mine * FIN, 1).reshape(16, 8, FOUT)
    grads = jnp.stack([grads[:, :, :LANES], grads[:, :, LANES:]], axis=1)
    grads = grads.reshape(32, 8, LANES)
    high = grads.astype(BF).astype(F32)
    low = grads - high
    swap = lambda x: jnp.concatenate([x[:, 4:], x[:, :4]], axis=1)
    first = iota((32, 8, LANES), 1) < 4
    even = jnp.where(first, high, swap(low))
    odd = jnp.where(first, swap(high), low)
    pieces = jnp.stack([even, odd], axis=1).reshape(PEERS, 8, LANES)
    wire = jnp.concatenate([main, pieces], axis=1)
    wire_ref[...] = wire.reshape(PEERS * WIDE, LANES).astype(BF)


def value_copies(part, bundles, value_ref, sems):
    own = pl.ds(part * HALF, HALF)
    return start_all(
        [(bundles[k].at[pl.ds(0, PACK), own], value_ref.at[k]) for k in range(FEATS)], sems
    )


def mean_copies(means, mean_ref, sems):
    return start_all([(means[k], mean_ref.at[k]) for k in range(FEATS - 1)], sems)


def dense_half(
    part, own_mean, mean_ref, value_ref, weight_ref, bias_ref, back_ref, index_ref, copies,
    halo_ref, hub_ref, out_ref, gmean_ref, ginput_ref, gpre_ref,
):
    chunk = CHUNK
    for i in range(HALF // chunk):
        here = slice(i * chunk, (i + 1) * chunk)
        whole = slice(part * HALF + i * chunk, part * HALF + (i + 1) * chunk)
        pre = jnp.tile(bias_ref[...], (1, chunk // LANES))
        for k in range(FEATS):
            mean = mean_ref[k - 1, :, here] if k else own_mean[:, here]
            both = jnp.concatenate([value_ref[k, :FIN, here], mean], axis=0)
            pre = pre + matmul(weight_ref[k], both).astype(BF).astype(F32)
        sigma = 1.0 / (1.0 + jnp.exp(-pre))
        out_ref[:, here] = (pre[:FIN] * sigma[:FIN]).astype(BF)
        slope = sigma * (1.0 + pre * (1.0 - sigma))
        gout = jnp.concatenate([value_ref[k, FIN:, here] for k in range(FEATS)], axis=0)
        gpre = (gout.astype(F32) * slope).astype(BF)
        gpre_ref[:, here] = gpre
        back = matmul(back_ref[...], gpre)
        ginput_ref[:, here] = back[:FIN]
        gmean_ref[:, here] = (back[FIN:] / index_ref[8:9, whole]).astype(BF)
    left = jnp.concatenate([value_ref[0, :FIN], own_mean[...], jnp.ones((16, HALF), BF)], axis=0)
    grads = matmul_nt(left, gpre_ref[...])
    for copy in copies:
        copy.wait()
    halos = matmul(gmean_ref[...], halo_ref[...])
    hubs = matmul(gmean_ref[...], hub_ref[...])
    return halos, hubs, grads


def first_dense_kernel(mine_ref, own_mean, index_ref, *refs):
    bundles, means, halo_hbm, hub_hbm = refs[:4], refs[4:7], refs[7], refs[8]
    out_ref, gmean_ref, ginput_ref, halo_acc, hub_acc, grad_acc = refs[9:15]
    weight_ref, bias_ref, back_ref, later_ref = refs[15:19]
    gpre_ref, halo_ref, hub_ref, pack_ref, value_ref, mean_ref = refs[19:25]
    pack_sems, value_sems, mean_sems, sems, later_sems = refs[25:]
    packs = start_all(
        [(bundles[k].at[pl.ds(PACK, 32)], pack_ref.at[k]) for k in range(FEATS)], pack_sems
    )
    ready = value_copies(0, bundles, value_ref, value_sems)
    ready = ready + mean_copies(means, mean_ref, mean_sems)
    copies = adjacency_copies(0, 4, halo_hbm, hub_hbm, halo_ref, hub_ref, sems)
    later = value_copies(1, bundles, later_ref, later_sems)
    for copy in packs:
        copy.wait()
    prepare_weights(mine_ref[0], pack_ref, weight_ref, bias_ref, back_ref)
    for copy in ready:
        copy.wait()
    halo_acc[...], hub_acc[...], grad_acc[...] = dense_half(
        0, own_mean, mean_ref, value_ref, weight_ref, bias_ref, back_ref, index_ref, copies,
        halo_ref, hub_ref, out_ref, gmean_ref, ginput_ref, gpre_ref,
    )
    for copy in later:
        copy.wait()


def later_dense_kernel(mine_ref, own_mean, index_ref, *refs):
    held_halo, held_hub, held_grad, weight_ref, bias_ref, back_ref, value_ref = refs[:7]
    means, halo_hbm, hub_hbm = refs[7:10], refs[10], refs[11]
    out_ref, gmean_ref, ginput_ref, wire_ref = refs[12:16]
    gpre_ref, halo_ref, hub_ref, halo_acc, hub_acc, grad_acc, mean_ref = refs[16:23]
    mean_sems, sems = refs[23:]
    ready = mean_copies(means, mean_ref, mean_sems)
    copies = adjacency_copies(1, 4, halo_hbm, hub_hbm, halo_ref, hub_ref, sems)
    for copy in ready:
        copy.wait()
    halos, hubs, grads = dense_half(
        1, own_mean, mean_ref, value_ref, weight_ref, bias_ref, back_ref, index_ref, copies,
        halo_ref, hub_ref, out_ref, gmean_ref, ginput_ref, gpre_ref,
    )
    halo_acc[...] = held_halo[...] + halos
    hub_acc[...] = held_hub[...] + hubs
    grad_acc[...] = held_grad[...] + grads
    ship_gradients(mine_ref[0], halo_acc, hub_acc, grad_acc, wire_ref)


ACCUMULATORS = [(FIN, HALO), (FIN, HUB_ALL), (PACK + 16, FOUT)]


def dense(part, mine, bundles, means, index, halo_adj, hub_adj, held):
    out_shape = [
        jax.ShapeDtypeStruct((FIN, HALF), BF),
        jax.ShapeDtypeStruct((FIN, HALF), BF),
        jax.ShapeDtypeStruct((FIN, HALF), F32),
    ]
    scratch = [
        pltpu.VMEM((FOUT, HALF), BF),
        pltpu.VMEM((HALF, HALO), BF),
        pltpu.VMEM((HALF, HUB_ALL), BF),
    ]
    remote = pltpu.VMEM((FEATS - 1, FIN, HALF), BF)
    value = pltpu.VMEM((FEATS, PACK, HALF), BF)
    if part == 0:
        out_shape += [pltpu.VMEM(shape, F32) for shape in ACCUMULATORS]
        out_shape += [
            pltpu.VMEM((FEATS, FOUT, PACK), BF),
            pltpu.VMEM((FOUT, LANES), F32),
            pltpu.VMEM((PACK, FOUT), BF),
            value,
        ]
        scratch += [pltpu.VMEM((FEATS, 32, NODES), BF), value, remote]
        counts = [4, 4, 3, 5, 4]
        far = keep_hbm(*bundles, *means[1:], halo_adj, hub_adj)
    else:
        out_shape += [jax.ShapeDtypeStruct((PEERS * WIDE, LANES), BF)]
        scratch += [pltpu.VMEM(shape, F32) for shape in ACCUMULATORS] + [remote]
        counts = [3, 5]
        far = keep_hbm(*means[1:], halo_adj, hub_adj)
    scratch += [pltpu.SemaphoreType.DMA((count,)) for count in counts]
    return pl.pallas_call(
        later_dense_kernel if part else first_dense_kernel,
        in_specs=[pl.BlockSpec(memory_space=pltpu.SMEM)]
        + in_vmem(2 + len(held))
        + in_hbm(len(far)),
        out_specs=in_vmem(len(out_shape)),
        out_shape=out_shape,
        scratch_shapes=scratch,
        compiler_params=params(),
        cost_estimate=cost(NODES * 2048 * 256, 6000000),
        name="dense",
    )(mine, means[0], index, *held, *far)


def back_kernel(
    ginput0, ginput1, gmean0, gmean1, out0, out1, adj_hbm, total_ref, out_ref, adj_ref, sems
):
    chunk = 512
    here = [pl.ds(i * chunk, chunk) for i in range(NODES // chunk)]
    blocks = start_all([(adj_hbm.at[:, i], adj_ref.at[:, i]) for i in here], sems)
    out_ref[:, :HALF] = out0[...]
    out_ref[:, HALF:] = out1[...]
    for i in range(NODES // chunk):
        blocks[i].wait()
        here = slice(i * chunk, (i + 1) * chunk)
        total = matmul(gmean0[...], adj_ref[:HALF, here])
        total = total + matmul(gmean1[...], adj_ref[HALF:, here])
        half = ginput0 if i * chunk < HALF else ginput1
        start = i * chunk % HALF
        total_ref[:, here] = total + half[:, start:start + chunk]


def local_back(ginputs, gmeans, outs, adj):
    return pl.pallas_call(
        back_kernel,
        in_specs=in_vmem(6) + in_hbm(1),
        out_specs=in_vmem(2),
        out_shape=[
            pltpu.VMEM((FIN, NODES), F32),
            jax.ShapeDtypeStruct((FIN, NODES), BF),
        ],
        scratch_shapes=[
            pltpu.VMEM((NODES, NODES), BF),
            pltpu.SemaphoreType.DMA((4,)),
        ],
        compiler_params=params(),
        cost_estimate=cost(2 * NODES * NODES * 256, 10000000),
        name="local_back",
    )(*ginputs, *gmeans, *outs, *keep_hbm(adj))


def reduce_kernel(wire_ref, sums_ref, bias_ref):
    wire = wire_ref[...].astype(F32).reshape(PEERS, WIDE, LANES)
    pieces = jnp.sum(wire[:, 16:], axis=0)
    half = pieces[:4] + pieces[4:]
    both = jnp.concatenate([half, half], axis=0)
    sums_ref[...] = jnp.broadcast_to(both[None], (PEERS // 2, 8, LANES)).reshape(
        PEERS * 4, LANES
    )
    tail = jnp.sum(wire[:, 8:16], axis=0)
    bias_ref[...] = tail[4:5, FIN:] + tail[5:6, FIN:]


def reduce_grads(wire):
    return pl.pallas_call(
        reduce_kernel,
        out_shape=[
            jax.ShapeDtypeStruct((PEERS * 4, LANES), F32),
            jax.ShapeDtypeStruct((1, FIN), F32),
        ],
        compiler_params=params(),
        in_specs=in_vmem(1),
        out_specs=in_vmem(2),
        cost_estimate=cost(1000000, 1000000),
        name="reduce_grads",
    )(wire)


def scatter_kernel(wire_ref, index_ref, total_ref, out_ref):
    wire = wire_ref[...].astype(F32).reshape(PEERS, WIDE, LANES)
    both = wire[:, :16].reshape(SLOTS, LANES).T
    back = jnp.concatenate([both[:FIN], both[FIN:]], axis=1).astype(BF)
    chunk = 256
    target = index_ref[0:1, :].astype(I32)
    node = iota((chunk, 2 * SLOTS), 0)
    for k in range(NODES // chunk):
        here = slice(k * chunk, (k + 1) * chunk)
        hot = (node == target - k * chunk).astype(F32).astype(BF)
        out_ref[:, here] = (total_ref[:, here] + matmul_nt(back, hot)).astype(BF)


def scatter_rows(wire, index, total):
    return pl.pallas_call(
        scatter_kernel,
        in_specs=in_vmem(3),
        out_specs=in_vmem(1)[0],
        out_shape=jax.ShapeDtypeStruct((FIN, NODES), BF),
        compiler_params=params(),
        cost_estimate=cost(2 * 2 * SLOTS * NODES * 256, 2000000),
        name="scatter_rows",
    )(wire, index, total)


def from_feat(value):
    shifted = [
        lax.ppermute(value, "feat", [(j, (j - k) % FEATS) for j in range(FEATS)])
        for k in range(1, FEATS)
    ]
    return [value] + shifted


def on_device(
    features,
    w_self,
    w_neigh,
    bias,
    grad_out,
    degree,
    tiles,
    tile_src,
    tile_dst,
    tile_count,
    halo_adj,
    send_rows,
    send_count,
    hub_adj,
    hub_local,
):
    feat = features.T
    gout = grad_out.T
    mine = lax.axis_index("feat").astype(I32).reshape(1)
    degree = degree.reshape(1, NODES)
    send = jnp.transpose(send_rows[0])
    wire, index, packed = front(
        hub_local, send, send_count, feat, gout, w_self, w_neigh, bias.reshape(1, FIN), degree
    )
    bundles = from_feat(packed)
    arrived = lax.all_to_all(wire, "dom", split_axis=0, concat_axis=0, tiled=True)
    local, adj = local_sum(tile_src, tile_dst, tile_count, tiles, packed)
    mean, *known = first_mean(arrived, halo_adj, hub_adj, local, index)
    mean, bundles = lax.optimization_barrier((mean, bundles))
    first = from_feat(mean)
    mean = later_mean(known, local, index)
    second = from_feat(mean)
    out0, gmean0, ginput0, *held = dense(0, mine, bundles, first, index, halo_adj, hub_adj, [])
    out1, gmean1, ginput1, wire = dense(1, mine, bundles, second, index, halo_adj, hub_adj, held)
    returned = lax.all_to_all(wire, "dom", split_axis=0, concat_axis=0, tiled=True)
    total, out = local_back([ginput0, ginput1], [gmean0, gmean1], [out0, out1], adj)
    returned, total = lax.optimization_barrier((returned, total))
    sums, grad_bias = reduce_grads(returned)
    shared = lax.all_to_all(sums, "dom", split_axis=0, concat_axis=0, tiled=True)
    grad_features = scatter_rows(returned, index, total)
    grads = shared.reshape(16, 2, 8, LANES).transpose(0, 2, 1, 3).reshape(PACK, FOUT)
    return (
        out.T,
        grad_features.T,
        grads[:FIN],
        grads[FIN:],
        grad_bias.reshape(FIN),
    )


def solution(mesh):
    in_specs = (
        P("dom", "feat"),
        P("feat", None),
        P("feat", None),
        P("feat"),
        P("dom", "feat"),
        P("dom"),
        P("dom", None, None),
        P("dom"),
        P("dom"),
        P("dom"),
        P("dom", None),
        P("dom", None, None),
        P("dom", None),
        P("dom", None),
        P("dom"),
    )
    out_specs = (P("dom", "feat"), P("dom", "feat"), P("feat", None), P("feat", None), P("feat"))
    return jax.shard_map(
        on_device, mesh=mesh, in_specs=in_specs, out_specs=out_specs, check_vma=False
    )
```

```python
import jax
import jax.numpy as jnp
from jax import lax
from jax.experimental import pallas as pl
from jax.experimental.pallas import tpu as pltpu
from jax.sharding import PartitionSpec as P

BF = jnp.bfloat16
F32 = jnp.float32
I32 = jnp.int32

PEERS = 64
FEATS = 4
SLOT = 24
HUBS = 4
ROWS = 16
WIDE = 24
LANES = 128
FIN = 64
FOUT = 256
NODES = 2048
BLOCK = 128
TILES = 128
HALO = PEERS * SLOT
HUB_ALL = PEERS * HUBS
BUNDLE = 144
WIDTH = 2048 + 128
PACK = 2 * FIN
HALF = NODES // 2
SLOTS = PEERS * ROWS
CHUNK = 256
NEAR = HALF // 2

def matmul(left, right):
    return lax.dot_general(
        left, right, (((1,), (0,)), ((), ())), preferred_element_type=F32
    )


def matmul_nt(left, right):
    return lax.dot_general(
        left, right, (((1,), (1,)), ((), ())), preferred_element_type=F32
    )


def params(mebibytes=24):
    return pltpu.CompilerParams(vmem_limit_bytes=mebibytes * 1024 * 1024)


def cost(flops, moved):
    return pl.CostEstimate(flops=flops, bytes_accessed=moved, transcendentals=0)


def in_vmem(count):
    return [pl.BlockSpec(memory_space=pltpu.VMEM)] * count


def in_hbm(count):
    return [pl.BlockSpec(memory_space=pltpu.HBM)] * count


def keep_hbm(*values):
    return [pltpu.with_memory_space_constraint(value, pltpu.HBM) for value in values]


def iota(shape, axis):
    return lax.broadcasted_iota(I32, shape, axis)


def pick_hubs():
    hub = iota((HUB_ALL, PEERS * 8), 0)
    place = iota((HUB_ALL, PEERS * 8), 1)
    same = (hub // HUBS == place // 8) & (hub % HUBS == place % 8)
    return same.astype(F32).astype(BF)


def start_all(pairs, sems):
    copies = [
        pltpu.make_async_copy(src, dst, sems.at[i]) for i, (src, dst) in enumerate(pairs)
    ]
    for copy in copies:
        copy.start()
    return copies


def slot_targets(hub_ref, send_ref, count_ref):
    slot = iota((SLOT, PEERS), 0)
    sent = jnp.where(slot < count_ref[...], send_ref[...], -1)
    place = iota((8, PEERS), 0)
    hubs = jnp.full((8, PEERS), -1, I32)
    for h in range(HUBS):
        hubs = jnp.where(place == h, hub_ref[h], hubs)
    rows = jnp.concatenate([sent, hubs], axis=0)
    high = lax.shift_right_arithmetic(rows, 6)
    low = rows - high * 64
    split = jnp.concatenate([high, low], axis=0).astype(F32).astype(BF)
    spread = (iota((PEERS, SLOTS), 0) == iota((PEERS, SLOTS), 1) // ROWS)
    wide = matmul(split, spread.astype(F32).astype(BF))
    wide = wide[:32] * 64.0 + wide[32:]
    mine = iota((ROWS, SLOTS), 0) == iota((ROWS, SLOTS), 1) % ROWS
    left = jnp.sum(jnp.where(mine, wide[:ROWS], 0.0), axis=0, keepdims=True)
    right = jnp.sum(jnp.where(mine, wide[ROWS:], 0.0), axis=0, keepdims=True)
    return jnp.concatenate([left, right], axis=1)


def bundle_kernel(
    feat_hbm, gout_hbm, self_hbm, neigh_hbm, bias_hbm, bundle_ref,
    self_ref, neigh_ref, bias_ref, sems,
):
    copies = start_all(
        [
            (self_hbm, self_ref),
            (neigh_hbm, neigh_ref),
            (bias_hbm, bias_ref),
            (feat_hbm, bundle_ref.at[pl.ds(0, FIN), pl.ds(0, NODES)]),
            (gout_hbm, bundle_ref.at[pl.ds(FIN, FIN), pl.ds(0, NODES)]),
        ],
        sems,
    )
    bundle_ref[:, NODES:] = jnp.zeros((BUNDLE, LANES), BF)
    for copy in copies[:3]:
        copy.wait()
    for i in range(4):
        rows = slice(16 * i, 16 * i + 16)
        bundle_ref[PACK:, FOUT * i:FOUT * (i + 1)] = self_ref[rows]
        bundle_ref[PACK:, FOUT * (i + 4):FOUT * (i + 5)] = neigh_ref[rows]
    bias = bias_ref[...]
    high = bias.astype(BF).astype(F32)
    middle = (bias - high).astype(BF).astype(F32)
    low = bias - high - middle
    place = iota((16, FIN), 0)
    parts = jnp.where(
        place == 0, high, jnp.where(place == 1, middle, jnp.where(place == 2, low, 0.0))
    )
    parts = jnp.concatenate([parts, jnp.zeros((16, LANES - FIN), F32)], axis=1).astype(BF)
    bundle_ref[PACK:, NODES:] = parts
    for copy in copies[3:]:
        copy.wait()


def bundle(*operands):
    return pl.pallas_call(
        bundle_kernel,
        in_specs=in_hbm(5),
        out_specs=in_vmem(1)[0],
        out_shape=pltpu.VMEM((BUNDLE, WIDTH), BF),
        scratch_shapes=[
            pltpu.VMEM((FIN, FOUT), BF),
            pltpu.VMEM((FIN, FOUT), BF),
            pltpu.VMEM((1, FIN), F32),
            pltpu.SemaphoreType.DMA((5,)),
        ],
        compiler_params=params(),
        cost_estimate=cost(1000000, 2000000),
        name="bundle",
    )(*keep_hbm(*operands))


def gather_kernel(
    hub_hbm, send_hbm, count_hbm, feat_hbm, degree_hbm, wire_ref, index_ref,
    hub_ref, send_ref, count_ref, feat_ref, degree_ref, sems,
):
    copies = start_all(
        [
            (hub_hbm, hub_ref),
            (send_hbm, send_ref),
            (count_hbm, count_ref),
            (degree_hbm, degree_ref),
            (feat_hbm, feat_ref),
        ],
        sems,
    )
    for copy in copies[:4]:
        copy.wait()
    both = slot_targets(hub_ref, send_ref, count_ref)
    index_ref[:8] = jnp.broadcast_to(both, (8, 2 * SLOTS))
    index_ref[8:] = jnp.broadcast_to(degree_ref[...].astype(F32), (8, NODES))
    copies[4].wait()
    step = 256
    total = jnp.zeros((FIN, 2 * SLOTS), F32)
    node = iota((step, 2 * SLOTS), 0).astype(F32).astype(BF)
    for k in range(NODES // step):
        target = (both - float(k * step)).astype(BF)
        hot = jnp.where(node == target, jnp.ones((), BF), jnp.zeros((), BF))
        total += matmul(feat_ref[:, k * step:(k + 1) * step], hot)
    stacked = jnp.concatenate([total[:, :SLOTS], total[:, SLOTS:]], axis=0)
    wire_ref[...] = stacked.T.astype(BF)


def gather_rows(*operands):
    return pl.pallas_call(
        gather_kernel,
        in_specs=in_hbm(5),
        out_specs=in_vmem(2),
        out_shape=[
            jax.ShapeDtypeStruct((SLOTS, LANES), BF),
            pltpu.VMEM((16, NODES), F32),
        ],
        scratch_shapes=[
            pltpu.SMEM((HUBS,), I32),
            pltpu.VMEM((SLOT, PEERS), I32),
            pltpu.VMEM((1, PEERS), I32),
            pltpu.VMEM((FIN, NODES), BF),
            pltpu.VMEM((1, NODES), I32),
            pltpu.SemaphoreType.DMA((5,)),
        ],
        compiler_params=params(),
        cost_estimate=cost(2 * 2 * SLOTS * NODES * 256, 1000000),
        name="gather_rows",
    )(*keep_hbm(*operands))


def local_kernel(
    count_ref, src_hbm, dst_hbm, tiles_hbm, feat_hbm, sum_ref, adj_hbm,
    src_ref, dst_ref, feat_ref, tiles_ref, adj_ref, sems, tile_sems, out_sems,
):
    small = start_all(
        [(src_hbm, src_ref), (dst_hbm, dst_ref), (feat_hbm, feat_ref)], sems
    )
    groups = tile_sems.shape[0]
    group = TILES // groups
    here = [pl.ds(g * group, group) for g in range(groups)]
    incoming = start_all([(tiles_hbm.at[g], tiles_ref.at[g]) for g in here], tile_sems)
    adj_ref[...] = jnp.zeros_like(adj_ref)
    for copy in small:
        copy.wait()
    for g in range(groups):
        incoming[g].wait()
        for j in range(group):
            t = g * group + j

            @pl.when(t < count_ref[0])
            def add():
                rows = pl.ds(pl.multiple_of(dst_ref[t] * BLOCK, BLOCK), BLOCK)
                cols = pl.ds(pl.multiple_of(src_ref[t] * BLOCK, BLOCK), BLOCK)
                adj_ref[rows, cols] += tiles_ref[t]

    width = 256
    here = [pl.ds(k * width, width) for k in range(NODES // width)]
    outgoing = start_all([(adj_ref.at[k], adj_hbm.at[k]) for k in here], out_sems)
    for k in range(NODES // width):
        part = adj_ref[k * width:(k + 1) * width, :]
        sum_ref[:, k * width:(k + 1) * width] = matmul_nt(feat_ref[...], part)
    for copy in outgoing:
        copy.wait()


def local_sum(src, dst, count, tiles, feat):
    return pl.pallas_call(
        local_kernel,
        in_specs=[pl.BlockSpec(memory_space=pltpu.SMEM)] + in_hbm(4),
        out_specs=in_vmem(1) + in_hbm(1),
        out_shape=[
            pltpu.VMEM((FIN, NODES), F32),
            pltpu.HBM((NODES, NODES), BF),
        ],
        scratch_shapes=[
            pltpu.SMEM((TILES,), I32),
            pltpu.SMEM((TILES,), I32),
            pltpu.VMEM((FIN, NODES), BF),
            pltpu.VMEM((TILES, BLOCK, BLOCK), BF),
            pltpu.VMEM((NODES, NODES), BF),
            pltpu.SemaphoreType.DMA((3,)),
            pltpu.SemaphoreType.DMA((8,)),
            pltpu.SemaphoreType.DMA((8,)),
        ],
        compiler_params=params(),
        cost_estimate=cost(2 * NODES * NODES * 256, 13000000),
        name="local_sum",
    )(count, *keep_hbm(src, dst, tiles, feat))


def adjacency_copies(start, rows, pieces, halo_hbm, hub_hbm, halo_ref, hub_ref, sems):
    piece = rows // pieces
    pairs = []
    for i in range(pieces):
        there = pl.ds(start + i * piece, piece)
        pairs.append((halo_hbm.at[there], halo_ref.at[pl.ds(i * piece, piece)]))
    pairs.append((hub_hbm.at[pl.ds(start, rows)], hub_ref))
    return start_all(pairs, sems)


def mean_part(start, column, rows, hubs, halo, hub, local_ref, index_ref, mean_ref):
    count = halo.shape[0]
    total = matmul(halo, rows) + matmul(hub, hubs)
    there = slice(start, start + count)
    total = total.T + local_ref[:, there]
    mean_ref[:, column:column + count] = (total / index_ref[8:9, there]).astype(BF)


def half_copies(part, halo_hbm, hub_hbm, halo_ref, hub_ref, sems):
    return [
        adjacency_copies(
            part * HALF + i * NEAR, NEAR, 1,
            halo_hbm, hub_hbm, halo_ref.at[i], hub_ref.at[i], sems.at[i],
        )
        for i in range(2)
    ]


def mean_half(part, copies, rows, hubs, halo_ref, hub_ref, local_ref, index_ref, mean_ref):
    for i in range(2):
        for copy in copies[i]:
            copy.wait()
        mean_part(
            part * HALF + i * NEAR, i * NEAR, rows, hubs, halo_ref[i], hub_ref[i],
            local_ref, index_ref, mean_ref,
        )


def first_mean_kernel(
    wire_ref, local_ref, index_ref, halo_hbm, hub_hbm, mean_ref, rows_ref, hubs_ref,
    halo_ref, hub_ref, sems,
):
    copies = half_copies(0, halo_hbm, hub_hbm, halo_ref, hub_ref, sems)
    wire = wire_ref[...].astype(F32).reshape(PEERS, ROWS, LANES)
    left = wire[:, :, :FIN]
    right = wire[:, :, FIN:]
    rows = jnp.concatenate([left, right[:, :8]], axis=1)
    rows_ref[...] = rows.reshape(HALO, FIN).astype(BF)
    owned = right[:, 8:].reshape(PEERS * 8, FIN).astype(BF)
    hubs_ref[...] = matmul(pick_hubs(), owned).astype(BF)
    mean_half(
        0, copies, rows_ref[...], hubs_ref[...], halo_ref, hub_ref, local_ref, index_ref, mean_ref
    )


HALF_SCRATCH = [
    pltpu.VMEM((2, NEAR, HALO), BF),
    pltpu.VMEM((2, NEAR, HUB_ALL), BF),
    pltpu.SemaphoreType.DMA((2, 2)),
]


def first_mean(wire, halo_adj, hub_adj, local, index):
    shapes = [(FIN, HALF), (HALO, FIN), (HUB_ALL, FIN)]
    return pl.pallas_call(
        first_mean_kernel,
        in_specs=in_vmem(3) + in_hbm(2),
        out_specs=in_vmem(len(shapes)),
        out_shape=[pltpu.VMEM(shape, BF) for shape in shapes],
        scratch_shapes=HALF_SCRATCH,
        compiler_params=params(),
        cost_estimate=cost(HALF * (HALO + HUB_ALL) * 512, 1000000),
        name="mean_rows",
    )(wire, local, index, *keep_hbm(halo_adj, hub_adj))


def later_mean_kernel(mine_ref, rows_ref, hubs_ref, local_ref, index_ref, *refs):
    halo_hbm, hub_hbm, bundles = refs[0], refs[1], refs[2:6]
    mean_ref, weight_ref, bias_ref, back_ref, value_ref = refs[6:11]
    halo_ref, hub_ref, sems, pack_ref, pack_sems, value_sems = refs[11:]
    copies = half_copies(1, halo_hbm, hub_hbm, halo_ref, hub_ref, sems)
    packs = start_all(
        [(bundles[k].at[pl.ds(PACK, 16)], pack_ref.at[k]) for k in range(FEATS)], pack_sems
    )
    values = value_copies(0, bundles, value_ref, value_sems)
    mean_half(
        1, copies, rows_ref[...], hubs_ref[...], halo_ref, hub_ref, local_ref, index_ref, mean_ref
    )
    for copy in packs:
        copy.wait()
    prepare_weights(mine_ref[0], pack_ref, weight_ref, bias_ref, back_ref)
    for copy in values:
        copy.wait()


def later_mean(mine, known, local, index, halo_adj, hub_adj, bundles):
    return pl.pallas_call(
        later_mean_kernel,
        in_specs=[pl.BlockSpec(memory_space=pltpu.SMEM)]
        + in_vmem(4)
        + in_hbm(2)
        + [pl.BlockSpec(memory_space=pl.ANY)]
        + in_hbm(FEATS - 1),
        out_specs=in_vmem(5),
        out_shape=[
            pltpu.VMEM((FIN, HALF), BF),
            pltpu.VMEM((FEATS, FOUT, PACK), BF),
            pltpu.VMEM((FOUT, LANES), F32),
            pltpu.VMEM((PACK, FOUT), BF),
            pltpu.VMEM((FEATS, PACK, HALF), BF),
        ],
        scratch_shapes=HALF_SCRATCH
        + [
            pltpu.VMEM((FEATS, 16, WIDTH), BF),
            pltpu.SemaphoreType.DMA((FEATS,)),
            pltpu.SemaphoreType.DMA((FEATS,)),
        ],
        compiler_params=params(),
        cost_estimate=cost(HALF * (HALO + HUB_ALL) * 512, 1000000),
        name="mean_rows",
    )(
        mine, *known, local, index, *keep_hbm(halo_adj, hub_adj),
        bundles[0], *keep_hbm(*bundles[1:]),
    )


def prepare_weights(mine, packs, weight_ref, bias_ref, back_ref):
    eye = iota((FIN, FIN), 0) == iota((FIN, FIN), 1)
    for k in range(FEATS):
        pieces = [
            packs[k, :, FOUT * i:FOUT * (i + 1)].astype(F32) for i in range(8)
        ]
        turned = jnp.concatenate(pieces, axis=0).T.astype(BF)
        for b in range(FEATS):
            place = lax.rem(b - mine + FEATS, FEATS)
            rows = pl.ds(pl.multiple_of(place * FIN, FIN), FIN)
            weight_ref[k, rows, :] = turned[b * FIN:(b + 1) * FIN]
        parts = packs[k, :, NODES:].astype(F32)
        row = parts[0:1, :FIN] + parts[1:2, :FIN] + parts[2:3, :FIN]
        column = jnp.sum(jnp.where(eye, row, 0.0), axis=1, keepdims=True)
        bias_ref[k * FIN:(k + 1) * FIN, :] = jnp.broadcast_to(column, (FIN, LANES))
    back_ref[...] = weight_ref[0].astype(F32).T.astype(BF)


def ship_gradients(mine, halo_acc, hub_acc, grad_acc, wire_ref):
    rows = halo_acc[...].T.reshape(PEERS, SLOT, FIN)
    hubs = matmul(hub_acc[...].astype(BF), pick_hubs()).T.reshape(PEERS, 8, FIN)
    row = grad_acc[2 * FIN:2 * FIN + 1, :FIN]
    high = row.astype(BF).astype(F32)
    place = iota((8, FIN), 0)
    extra = jnp.where(place == 4, high, jnp.where(place == 5, row - high, 0.0))
    hubs = hubs + extra[None]
    right = jnp.concatenate([rows[:, 16:], hubs], axis=1)
    main = jnp.concatenate([rows[:, :16], right], axis=2)
    grads = pltpu.roll(grad_acc[:2 * FIN, :], mine * FIN, 1).reshape(16, 8, FOUT)
    grads = jnp.stack([grads[:, :, :LANES], grads[:, :, LANES:]], axis=1)
    grads = grads.reshape(32, 8, LANES)
    high = grads.astype(BF).astype(F32)
    low = grads - high
    swap = lambda x: jnp.concatenate([x[:, 4:], x[:, :4]], axis=1)
    first = iota((32, 8, LANES), 1) < 4
    even = jnp.where(first, high, swap(low))
    odd = jnp.where(first, swap(high), low)
    pieces = jnp.stack([even, odd], axis=1).reshape(PEERS, 8, LANES)
    wire = jnp.concatenate([main, pieces], axis=1)
    wire_ref[...] = wire.reshape(PEERS * WIDE, LANES).astype(BF)


def value_copies(part, bundles, value_ref, sems):
    own = pl.ds(part * HALF, HALF)
    return start_all(
        [(bundles[k].at[pl.ds(0, PACK), own], value_ref.at[k]) for k in range(FEATS)], sems
    )


def dense_half(
    part, means, value_ref, weight_ref, bias_ref, back_ref, index_ref, copies,
    halo_ref, hub_ref, out_ref, gmean_ref, ginput_ref, gpre_ref,
):
    chunk = CHUNK
    for i in range(HALF // chunk):
        here = slice(i * chunk, (i + 1) * chunk)
        whole = slice(part * HALF + i * chunk, part * HALF + (i + 1) * chunk)
        pre = jnp.tile(bias_ref[...], (1, chunk // LANES))
        for k in range(FEATS):
            both = jnp.concatenate([value_ref[k, :FIN, here], means[k][:, here]], axis=0)
            pre = pre + matmul(weight_ref[k], both).astype(BF).astype(F32)
        sigma = 0.5 * jnp.tanh(0.5 * pre) + 0.5
        out_ref[:, here] = (pre[:FIN] * sigma[:FIN]).astype(BF)
        slope = sigma * (1.0 + pre * (1.0 - sigma))
        gout = jnp.concatenate([value_ref[k, FIN:, here] for k in range(FEATS)], axis=0)
        gpre = (gout.astype(F32) * slope).astype(BF)
        gpre_ref[:, here] = gpre
        back = matmul(back_ref[...], gpre)
        ginput_ref[:, here] = back[:FIN]
        gmean_ref[:, here] = (back[FIN:] / index_ref[8:9, whole]).astype(BF)
    left = jnp.concatenate([value_ref[0, :FIN], means[0][...], jnp.ones((16, HALF), BF)], axis=0)
    grads = matmul_nt(left, gpre_ref[...])
    for copy in copies:
        copy.wait()
    halos = matmul(gmean_ref[...], halo_ref[...])
    hubs = matmul(gmean_ref[...], hub_ref[...])
    return halos, hubs, grads


def first_dense_kernel(*refs):
    means, index_ref = refs[:4], refs[4]
    weight_ref, bias_ref, back_ref, value_ref = refs[5:9]
    bundles, halo_hbm, hub_hbm = refs[9:13], refs[13], refs[14]
    out_ref, gmean_ref, ginput_ref, halo_acc, hub_acc, grad_acc, later_ref = refs[15:22]
    gpre_ref, halo_ref, hub_ref, sems, later_sems = refs[22:]
    copies = adjacency_copies(0, HALF, 4, halo_hbm, hub_hbm, halo_ref, hub_ref, sems)
    later = value_copies(1, bundles, later_ref, later_sems)
    halo_acc[...], hub_acc[...], grad_acc[...] = dense_half(
        0, means, value_ref, weight_ref, bias_ref, back_ref, index_ref, copies,
        halo_ref, hub_ref, out_ref, gmean_ref, ginput_ref, gpre_ref,
    )
    for copy in later:
        copy.wait()


def later_dense_kernel(mine_ref, *refs):
    means, index_ref = refs[:4], refs[4]
    weight_ref, bias_ref, back_ref, value_ref = refs[5:9]
    held_halo, held_hub, held_grad, halo_hbm, hub_hbm = refs[9:14]
    out_ref, gmean_ref, ginput_ref, wire_ref = refs[14:18]
    gpre_ref, halo_ref, hub_ref, halo_acc, hub_acc, grad_acc, sems = refs[18:]
    copies = adjacency_copies(HALF, HALF, 4, halo_hbm, hub_hbm, halo_ref, hub_ref, sems)
    halos, hubs, grads = dense_half(
        1, means, value_ref, weight_ref, bias_ref, back_ref, index_ref, copies,
        halo_ref, hub_ref, out_ref, gmean_ref, ginput_ref, gpre_ref,
    )
    halo_acc[...] = held_halo[...] + halos
    hub_acc[...] = held_hub[...] + hubs
    grad_acc[...] = held_grad[...] + grads
    ship_gradients(mine_ref[0], halo_acc, hub_acc, grad_acc, wire_ref)


ACCUMULATORS = [(FIN, HALO), (FIN, HUB_ALL), (PACK + 16, FOUT)]
HALVES = [
    jax.ShapeDtypeStruct((FIN, HALF), BF),
    jax.ShapeDtypeStruct((FIN, HALF), BF),
    jax.ShapeDtypeStruct((FIN, HALF), F32),
]
ADJACENCY = [
    pltpu.VMEM((FOUT, HALF), BF),
    pltpu.VMEM((HALF, HALO), BF),
    pltpu.VMEM((HALF, HUB_ALL), BF),
]


def first_dense(means, index, weights, value, bundles, halo_adj, hub_adj):
    out_shape = HALVES + [pltpu.VMEM(shape, F32) for shape in ACCUMULATORS]
    out_shape += [pltpu.VMEM((FEATS, PACK, HALF), BF)]
    return pl.pallas_call(
        first_dense_kernel,
        in_specs=in_vmem(9) + [pl.BlockSpec(memory_space=pl.ANY)] + in_hbm(FEATS + 1),
        out_specs=in_vmem(len(out_shape)),
        out_shape=out_shape,
        scratch_shapes=ADJACENCY
        + [pltpu.SemaphoreType.DMA((5,)), pltpu.SemaphoreType.DMA((FEATS,))],
        compiler_params=params(),
        cost_estimate=cost(NODES * 2048 * 256, 6000000),
        name="dense",
    )(*means, index, *weights, value, bundles[0], *keep_hbm(*bundles[1:], halo_adj, hub_adj))


def later_dense(mine, means, index, weights, value, held, halo_adj, hub_adj):
    out_shape = HALVES + [jax.ShapeDtypeStruct((PEERS * WIDE, LANES), BF)]
    return pl.pallas_call(
        later_dense_kernel,
        in_specs=[pl.BlockSpec(memory_space=pltpu.SMEM)] + in_vmem(12) + in_hbm(2),
        out_specs=in_vmem(len(out_shape)),
        out_shape=out_shape,
        scratch_shapes=ADJACENCY
        + [pltpu.VMEM(shape, F32) for shape in ACCUMULATORS]
        + [pltpu.SemaphoreType.DMA((5,))],
        compiler_params=params(),
        cost_estimate=cost(NODES * 2048 * 256, 6000000),
        name="dense",
    )(mine, *means, index, *weights, value, *held, *keep_hbm(halo_adj, hub_adj))


def back_kernel(
    ginput0, ginput1, gmean0, gmean1, out0, out1, adj_hbm, total_ref, out_ref, adj_ref, sems
):
    chunk = 512
    here = [pl.ds(i * chunk, chunk) for i in range(NODES // chunk)]
    blocks = start_all([(adj_hbm.at[:, i], adj_ref.at[:, i]) for i in here], sems)
    out_ref[:, :HALF] = out0[...]
    out_ref[:, HALF:] = out1[...]
    for i in range(NODES // chunk):
        blocks[i].wait()
        here = slice(i * chunk, (i + 1) * chunk)
        total = matmul(gmean0[...], adj_ref[:HALF, here])
        total = total + matmul(gmean1[...], adj_ref[HALF:, here])
        half = ginput0 if i * chunk < HALF else ginput1
        start = i * chunk % HALF
        total_ref[:, here] = total + half[:, start:start + chunk]


def local_back(ginputs, gmeans, outs, adj):
    return pl.pallas_call(
        back_kernel,
        in_specs=in_vmem(6) + in_hbm(1),
        out_specs=in_vmem(2),
        out_shape=[
            pltpu.VMEM((FIN, NODES), F32),
            jax.ShapeDtypeStruct((FIN, NODES), BF),
        ],
        scratch_shapes=[
            pltpu.VMEM((NODES, NODES), BF),
            pltpu.SemaphoreType.DMA((4,)),
        ],
        compiler_params=params(),
        cost_estimate=cost(2 * NODES * NODES * 256, 10000000),
        name="local_back",
    )(*ginputs, *gmeans, *outs, *keep_hbm(adj))


def reduce_kernel(wire_ref, sums_ref, bias_ref):
    wire = wire_ref[...].astype(F32).reshape(PEERS, WIDE, LANES)
    pieces = jnp.sum(wire[:, 16:], axis=0)
    half = pieces[:4] + pieces[4:]
    both = jnp.concatenate([half, half], axis=0)
    sums_ref[...] = jnp.broadcast_to(both[None], (PEERS // 2, 8, LANES)).reshape(
        PEERS * 4, LANES
    )
    tail = jnp.sum(wire[:, 8:16], axis=0)
    bias_ref[...] = tail[4:5, FIN:] + tail[5:6, FIN:]


def reduce_grads(wire):
    return pl.pallas_call(
        reduce_kernel,
        out_shape=[
            jax.ShapeDtypeStruct((PEERS * 4, LANES), F32),
            jax.ShapeDtypeStruct((1, FIN), F32),
        ],
        compiler_params=params(),
        in_specs=in_vmem(1),
        out_specs=in_vmem(2),
        cost_estimate=cost(1000000, 1000000),
        name="reduce_grads",
    )(wire)


def scatter_kernel(wire_ref, index_ref, total_ref, out_ref):
    wire = wire_ref[...].astype(F32).reshape(PEERS, WIDE, LANES)
    both = wire[:, :16].reshape(SLOTS, LANES).T
    back = jnp.concatenate([both[:FIN], both[FIN:]], axis=1).astype(BF)
    chunk = 256
    target = index_ref[0:1, :].astype(I32)
    node = iota((chunk, 2 * SLOTS), 0)
    for k in range(NODES // chunk):
        here = slice(k * chunk, (k + 1) * chunk)
        hot = (node == target - k * chunk).astype(F32).astype(BF)
        out_ref[:, here] = (total_ref[:, here] + matmul_nt(back, hot)).astype(BF)


def scatter_rows(wire, index, total):
    return pl.pallas_call(
        scatter_kernel,
        in_specs=in_vmem(3),
        out_specs=in_vmem(1)[0],
        out_shape=jax.ShapeDtypeStruct((FIN, NODES), BF),
        compiler_params=params(),
        cost_estimate=cost(2 * 2 * SLOTS * NODES * 256, 2000000),
        name="scatter_rows",
    )(wire, index, total)


def from_feat(value):
    shifted = [
        lax.ppermute(value, "feat", [(j, (j - k) % FEATS) for j in range(FEATS)])
        for k in range(1, FEATS)
    ]
    return [value] + shifted


def on_device(
    features,
    w_self,
    w_neigh,
    bias,
    grad_out,
    degree,
    tiles,
    tile_src,
    tile_dst,
    tile_count,
    halo_adj,
    send_rows,
    send_count,
    hub_adj,
    hub_local,
):
    feat = features.T
    gout = grad_out.T
    mine = lax.axis_index("feat").astype(I32).reshape(1)
    degree = degree.reshape(1, NODES)
    send = jnp.transpose(send_rows[0])
    packed = bundle(feat, gout, w_self, w_neigh, bias.reshape(1, FIN))
    packed, feat = lax.optimization_barrier((packed, feat))
    bundles = from_feat(packed)
    wire, index = gather_rows(hub_local, send, send_count, feat, degree)
    arrived = lax.all_to_all(wire, "dom", split_axis=0, concat_axis=0, tiled=True)
    local, adj = local_sum(tile_src, tile_dst, tile_count, tiles, feat)
    mean, *known = first_mean(arrived, halo_adj, hub_adj, local, index)
    mean, bundles = lax.optimization_barrier((mean, bundles))
    first = from_feat(mean)
    mean, *weights, value = later_mean(
        mine, known, local, index, halo_adj, hub_adj, bundles
    )
    second = from_feat(mean)
    out0, gmean0, ginput0, *held, value = first_dense(
        first, index, weights, value, bundles, halo_adj, hub_adj
    )
    out1, gmean1, ginput1, wire = later_dense(
        mine, second, index, weights, value, held, halo_adj, hub_adj
    )
    returned = lax.all_to_all(wire, "dom", split_axis=0, concat_axis=0, tiled=True)
    total, out = local_back([ginput0, ginput1], [gmean0, gmean1], [out0, out1], adj)
    returned, total = lax.optimization_barrier((returned, total))
    sums, grad_bias = reduce_grads(returned)
    shared = lax.all_to_all(sums, "dom", split_axis=0, concat_axis=0, tiled=True)
    grad_features = scatter_rows(returned, index, total)
    grads = shared.reshape(16, 2, 8, LANES).transpose(0, 2, 1, 3).reshape(PACK, FOUT)
    return (
        out.T,
        grad_features.T,
        grads[:FIN],
        grads[FIN:],
        grad_bias.reshape(FIN),
    )


def solution(mesh):
    in_specs = (
        P("dom", "feat"),
        P("feat", None),
        P("feat", None),
        P("feat"),
        P("dom", "feat"),
        P("dom"),
        P("dom", None, None),
        P("dom"),
        P("dom"),
        P("dom"),
        P("dom", None),
        P("dom", None, None),
        P("dom", None),
        P("dom", None),
        P("dom"),
    )
    out_specs = (P("dom", "feat"), P("dom", "feat"), P("feat", None), P("feat", None), P("feat"))
    return jax.shard_map(
        on_device, mesh=mesh, in_specs=in_specs, out_specs=out_specs, check_vma=False
    )
```

```python
import jax
import jax.numpy as jnp
from jax import lax
from jax.experimental import pallas as pl
from jax.experimental.pallas import tpu as pltpu
from jax.sharding import PartitionSpec as P

BF = jnp.bfloat16
F32 = jnp.float32
I32 = jnp.int32

PEERS = 64
FEATS = 4
SLOT = 24
HUBS = 4
ROWS = 16
WIDE = 24
LANES = 128
FIN = 64
FOUT = 256
NODES = 2048
BLOCK = 128
TILES = 128
HALO = PEERS * SLOT
HUB_ALL = PEERS * HUBS
BUNDLE = 144
WIDTH = 2048 + 128
PACK = 2 * FIN
SIZES = (1280, 768)
STARTS = (0, 1280)
SLOTS = PEERS * ROWS
CHUNK = 256

def matmul(left, right):
    return lax.dot_general(
        left, right, (((1,), (0,)), ((), ())), preferred_element_type=F32
    )


def matmul_nt(left, right):
    return lax.dot_general(
        left, right, (((1,), (1,)), ((), ())), preferred_element_type=F32
    )


def params(mebibytes=24):
    return pltpu.CompilerParams(vmem_limit_bytes=mebibytes * 1024 * 1024)


def cost(flops, moved):
    return pl.CostEstimate(flops=flops, bytes_accessed=moved, transcendentals=0)


def in_vmem(count):
    return [pl.BlockSpec(memory_space=pltpu.VMEM)] * count


def in_hbm(count):
    return [pl.BlockSpec(memory_space=pltpu.HBM)] * count


def keep_hbm(*values):
    return [pltpu.with_memory_space_constraint(value, pltpu.HBM) for value in values]


def iota(shape, axis):
    return lax.broadcasted_iota(I32, shape, axis)


def pick_hubs():
    hub = iota((HUB_ALL, PEERS * 8), 0)
    place = iota((HUB_ALL, PEERS * 8), 1)
    same = (hub // HUBS == place // 8) & (hub % HUBS == place % 8)
    return same.astype(F32).astype(BF)


def start_all(pairs, sems):
    copies = [
        pltpu.make_async_copy(src, dst, sems.at[i]) for i, (src, dst) in enumerate(pairs)
    ]
    for copy in copies:
        copy.start()
    return copies


def slot_targets(hub_ref, send_ref, count_ref):
    slot = iota((SLOT, PEERS), 0)
    sent = jnp.where(slot < count_ref[...], send_ref[...], -1)
    place = iota((8, PEERS), 0)
    hubs = jnp.full((8, PEERS), -1, I32)
    for h in range(HUBS):
        hubs = jnp.where(place == h, hub_ref[h], hubs)
    rows = jnp.concatenate([sent, hubs], axis=0)
    high = lax.shift_right_arithmetic(rows, 6)
    low = rows - high * 64
    split = jnp.concatenate([high, low], axis=0).astype(F32).astype(BF)
    spread = (iota((PEERS, SLOTS), 0) == iota((PEERS, SLOTS), 1) // ROWS)
    wide = matmul(split, spread.astype(F32).astype(BF))
    wide = wide[:32] * 64.0 + wide[32:]
    mine = iota((ROWS, SLOTS), 0) == iota((ROWS, SLOTS), 1) % ROWS
    left = jnp.sum(jnp.where(mine, wide[:ROWS], 0.0), axis=0, keepdims=True)
    right = jnp.sum(jnp.where(mine, wide[ROWS:], 0.0), axis=0, keepdims=True)
    return jnp.concatenate([left, right], axis=1)


def bundle_kernel(
    feat_hbm, gout_hbm, self_hbm, neigh_hbm, bias_hbm, bundle_ref,
    self_ref, neigh_ref, bias_ref, sems,
):
    copies = start_all(
        [
            (self_hbm, self_ref),
            (neigh_hbm, neigh_ref),
            (bias_hbm, bias_ref),
            (feat_hbm, bundle_ref.at[pl.ds(0, FIN), pl.ds(0, NODES)]),
            (gout_hbm, bundle_ref.at[pl.ds(FIN, FIN), pl.ds(0, NODES)]),
        ],
        sems,
    )
    bundle_ref[:, NODES:] = jnp.zeros((BUNDLE, LANES), BF)
    for copy in copies[:3]:
        copy.wait()
    for i in range(4):
        rows = slice(16 * i, 16 * i + 16)
        bundle_ref[PACK:, FOUT * i:FOUT * (i + 1)] = self_ref[rows]
        bundle_ref[PACK:, FOUT * (i + 4):FOUT * (i + 5)] = neigh_ref[rows]
    bias = bias_ref[...]
    high = bias.astype(BF).astype(F32)
    middle = (bias - high).astype(BF).astype(F32)
    low = bias - high - middle
    place = iota((16, FIN), 0)
    parts = jnp.where(
        place == 0, high, jnp.where(place == 1, middle, jnp.where(place == 2, low, 0.0))
    )
    parts = jnp.concatenate([parts, jnp.zeros((16, LANES - FIN), F32)], axis=1).astype(BF)
    bundle_ref[PACK:, NODES:] = parts
    for copy in copies[3:]:
        copy.wait()


def bundle(*operands):
    return pl.pallas_call(
        bundle_kernel,
        in_specs=in_hbm(5),
        out_specs=in_vmem(1)[0],
        out_shape=pltpu.VMEM((BUNDLE, WIDTH), BF),
        scratch_shapes=[
            pltpu.VMEM((FIN, FOUT), BF),
            pltpu.VMEM((FIN, FOUT), BF),
            pltpu.VMEM((1, FIN), F32),
            pltpu.SemaphoreType.DMA((5,)),
        ],
        compiler_params=params(),
        cost_estimate=cost(1000000, 2000000),
        name="bundle",
    )(*keep_hbm(*operands))


def gather_kernel(
    hub_hbm, send_hbm, count_hbm, feat_hbm, degree_hbm, wire_ref, index_ref,
    hub_ref, send_ref, count_ref, feat_ref, degree_ref, sems,
):
    copies = start_all(
        [
            (hub_hbm, hub_ref),
            (send_hbm, send_ref),
            (count_hbm, count_ref),
            (degree_hbm, degree_ref),
            (feat_hbm, feat_ref),
        ],
        sems,
    )
    for copy in copies[:4]:
        copy.wait()
    both = slot_targets(hub_ref, send_ref, count_ref)
    index_ref[:8] = jnp.broadcast_to(both, (8, 2 * SLOTS))
    index_ref[8:] = jnp.broadcast_to(degree_ref[...].astype(F32), (8, NODES))
    copies[4].wait()
    step = 256
    total = jnp.zeros((FIN, 2 * SLOTS), F32)
    node = iota((step, 2 * SLOTS), 0).astype(F32).astype(BF)
    for k in range(NODES // step):
        target = (both - float(k * step)).astype(BF)
        hot = jnp.where(node == target, jnp.ones((), BF), jnp.zeros((), BF))
        total += matmul(feat_ref[:, k * step:(k + 1) * step], hot)
    stacked = jnp.concatenate([total[:, :SLOTS], total[:, SLOTS:]], axis=0)
    wire_ref[...] = stacked.T.astype(BF)


def gather_rows(*operands):
    return pl.pallas_call(
        gather_kernel,
        in_specs=in_hbm(5),
        out_specs=in_vmem(2),
        out_shape=[
            jax.ShapeDtypeStruct((SLOTS, LANES), BF),
            pltpu.VMEM((16, NODES), F32),
        ],
        scratch_shapes=[
            pltpu.SMEM((HUBS,), I32),
            pltpu.VMEM((SLOT, PEERS), I32),
            pltpu.VMEM((1, PEERS), I32),
            pltpu.VMEM((FIN, NODES), BF),
            pltpu.VMEM((1, NODES), I32),
            pltpu.SemaphoreType.DMA((5,)),
        ],
        compiler_params=params(),
        cost_estimate=cost(2 * 2 * SLOTS * NODES * 256, 1000000),
        name="gather_rows",
    )(*keep_hbm(*operands))


def local_kernel(
    count_ref, src_hbm, dst_hbm, tiles_hbm, feat_hbm, sum_ref, adj_hbm,
    src_ref, dst_ref, feat_ref, tiles_ref, adj_ref, sems, tile_sems, out_sems,
):
    small = start_all(
        [(src_hbm, src_ref), (dst_hbm, dst_ref), (feat_hbm, feat_ref)], sems
    )
    groups = tile_sems.shape[0]
    group = TILES // groups
    here = [pl.ds(g * group, group) for g in range(groups)]
    incoming = start_all([(tiles_hbm.at[g], tiles_ref.at[g]) for g in here], tile_sems)
    adj_ref[...] = jnp.zeros_like(adj_ref)
    for copy in small:
        copy.wait()
    for g in range(groups):
        incoming[g].wait()
        for j in range(group):
            t = g * group + j

            @pl.when(t < count_ref[0])
            def add():
                rows = pl.ds(pl.multiple_of(dst_ref[t] * BLOCK, BLOCK), BLOCK)
                cols = pl.ds(pl.multiple_of(src_ref[t] * BLOCK, BLOCK), BLOCK)
                adj_ref[rows, cols] += tiles_ref[t]

    width = 256
    here = [pl.ds(k * width, width) for k in range(NODES // width)]
    outgoing = start_all([(adj_ref.at[k], adj_hbm.at[k]) for k in here], out_sems)
    for k in range(NODES // width):
        part = adj_ref[k * width:(k + 1) * width, :]
        sum_ref[:, k * width:(k + 1) * width] = matmul_nt(feat_ref[...], part)
    for copy in outgoing:
        copy.wait()


def local_sum(src, dst, count, tiles, feat):
    return pl.pallas_call(
        local_kernel,
        in_specs=[pl.BlockSpec(memory_space=pltpu.SMEM)] + in_hbm(4),
        out_specs=in_vmem(1) + in_hbm(1),
        out_shape=[
            pltpu.VMEM((FIN, NODES), F32),
            pltpu.HBM((NODES, NODES), BF),
        ],
        scratch_shapes=[
            pltpu.SMEM((TILES,), I32),
            pltpu.SMEM((TILES,), I32),
            pltpu.VMEM((FIN, NODES), BF),
            pltpu.VMEM((TILES, BLOCK, BLOCK), BF),
            pltpu.VMEM((NODES, NODES), BF),
            pltpu.SemaphoreType.DMA((3,)),
            pltpu.SemaphoreType.DMA((8,)),
            pltpu.SemaphoreType.DMA((8,)),
        ],
        compiler_params=params(),
        cost_estimate=cost(2 * NODES * NODES * 256, 13000000),
        name="local_sum",
    )(count, *keep_hbm(src, dst, tiles, feat))


def adjacency_copies(start, rows, pieces, halo_hbm, hub_hbm, halo_ref, hub_ref, sems):
    piece = rows // pieces
    pairs = []
    for i in range(pieces):
        there = pl.ds(start + i * piece, piece)
        pairs.append((halo_hbm.at[there], halo_ref.at[pl.ds(i * piece, piece)]))
    pairs.append((hub_hbm.at[pl.ds(start, rows)], hub_ref))
    return start_all(pairs, sems)


def mean_part(start, column, rows, hubs, halo, hub, local_ref, index_ref, mean_ref):
    count = halo.shape[0]
    total = matmul(halo, rows) + matmul(hub, hubs)
    there = slice(start, start + count)
    total = total.T + local_ref[:, there]
    mean_ref[:, column:column + count] = (total / index_ref[8:9, there]).astype(BF)


def half_copies(part, halo_hbm, hub_hbm, halo_ref, hub_ref, sems):
    near = SIZES[part] // 2
    return [
        adjacency_copies(
            STARTS[part] + i * near, near, 1,
            halo_hbm, hub_hbm, halo_ref.at[i], hub_ref.at[i], sems.at[i],
        )
        for i in range(2)
    ]


def mean_half(part, copies, rows, hubs, halo_ref, hub_ref, local_ref, index_ref, mean_ref):
    near = SIZES[part] // 2
    for i in range(2):
        for copy in copies[i]:
            copy.wait()
        mean_part(
            STARTS[part] + i * near, i * near, rows, hubs, halo_ref[i], hub_ref[i],
            local_ref, index_ref, mean_ref,
        )


def first_mean_kernel(
    wire_ref, local_ref, index_ref, halo_hbm, hub_hbm, mean_ref, rows_ref, hubs_ref,
    halo_ref, hub_ref, sems,
):
    copies = half_copies(0, halo_hbm, hub_hbm, halo_ref, hub_ref, sems)
    wire = wire_ref[...].astype(F32).reshape(PEERS, ROWS, LANES)
    left = wire[:, :, :FIN]
    right = wire[:, :, FIN:]
    rows = jnp.concatenate([left, right[:, :8]], axis=1)
    rows_ref[...] = rows.reshape(HALO, FIN).astype(BF)
    owned = right[:, 8:].reshape(PEERS * 8, FIN).astype(BF)
    hubs_ref[...] = matmul(pick_hubs(), owned).astype(BF)
    mean_half(
        0, copies, rows_ref[...], hubs_ref[...], halo_ref, hub_ref, local_ref, index_ref, mean_ref
    )


def half_scratch(part):
    near = SIZES[part] // 2
    return [
        pltpu.VMEM((2, near, HALO), BF),
        pltpu.VMEM((2, near, HUB_ALL), BF),
        pltpu.SemaphoreType.DMA((2, 2)),
    ]


def first_mean(wire, halo_adj, hub_adj, local, index):
    shapes = [(FIN, SIZES[0]), (HALO, FIN), (HUB_ALL, FIN)]
    return pl.pallas_call(
        first_mean_kernel,
        in_specs=in_vmem(3) + in_hbm(2),
        out_specs=in_vmem(len(shapes)),
        out_shape=[pltpu.VMEM(shape, BF) for shape in shapes],
        scratch_shapes=half_scratch(0),
        compiler_params=params(),
        cost_estimate=cost(1024 * (HALO + HUB_ALL) * 512, 1000000),
        name="mean_rows",
    )(wire, local, index, *keep_hbm(halo_adj, hub_adj))


def later_mean_kernel(mine_ref, rows_ref, hubs_ref, local_ref, index_ref, *refs):
    halo_hbm, hub_hbm, bundles = refs[0], refs[1], refs[2:6]
    mean_ref, weight_ref, bias_ref, back_ref, value_ref = refs[6:11]
    halo_ref, hub_ref, sems, pack_ref, pack_sems, value_sems = refs[11:]
    copies = half_copies(1, halo_hbm, hub_hbm, halo_ref, hub_ref, sems)
    packs = start_all(
        [(bundles[k].at[pl.ds(PACK, 16)], pack_ref.at[k]) for k in range(FEATS)], pack_sems
    )
    values = value_copies(0, bundles, value_ref, value_sems)
    mean_half(
        1, copies, rows_ref[...], hubs_ref[...], halo_ref, hub_ref, local_ref, index_ref, mean_ref
    )
    for copy in packs:
        copy.wait()
    prepare_weights(mine_ref[0], pack_ref, weight_ref, bias_ref, back_ref)
    for copy in values:
        copy.wait()


def later_mean(mine, known, local, index, halo_adj, hub_adj, bundles):
    return pl.pallas_call(
        later_mean_kernel,
        in_specs=[pl.BlockSpec(memory_space=pltpu.SMEM)]
        + in_vmem(4)
        + in_hbm(2)
        + [pl.BlockSpec(memory_space=pl.ANY)]
        + in_hbm(FEATS - 1),
        out_specs=in_vmem(5),
        out_shape=[
            pltpu.VMEM((FIN, SIZES[1]), BF),
            pltpu.VMEM((FEATS, FOUT, PACK), BF),
            pltpu.VMEM((FOUT, LANES), F32),
            pltpu.VMEM((PACK, FOUT), BF),
            pltpu.VMEM((FEATS, PACK, SIZES[0]), BF),
        ],
        scratch_shapes=half_scratch(1)
        + [
            pltpu.VMEM((FEATS, 16, WIDTH), BF),
            pltpu.SemaphoreType.DMA((FEATS,)),
            pltpu.SemaphoreType.DMA((FEATS,)),
        ],
        compiler_params=params(),
        cost_estimate=cost(1024 * (HALO + HUB_ALL) * 512, 1000000),
        name="mean_rows",
    )(
        mine, *known, local, index, *keep_hbm(halo_adj, hub_adj),
        bundles[0], *keep_hbm(*bundles[1:]),
    )


def prepare_weights(mine, packs, weight_ref, bias_ref, back_ref):
    eye = iota((FIN, FIN), 0) == iota((FIN, FIN), 1)
    for k in range(FEATS):
        pieces = [
            packs[k, :, FOUT * i:FOUT * (i + 1)].astype(F32) for i in range(8)
        ]
        turned = jnp.concatenate(pieces, axis=0).T.astype(BF)
        for b in range(FEATS):
            place = lax.rem(b - mine + FEATS, FEATS)
            rows = pl.ds(pl.multiple_of(place * FIN, FIN), FIN)
            weight_ref[k, rows, :] = turned[b * FIN:(b + 1) * FIN]
        parts = packs[k, :, NODES:].astype(F32)
        row = parts[0:1, :FIN] + parts[1:2, :FIN] + parts[2:3, :FIN]
        column = jnp.sum(jnp.where(eye, row, 0.0), axis=1, keepdims=True)
        bias_ref[k * FIN:(k + 1) * FIN, :] = jnp.broadcast_to(column, (FIN, LANES))
    back_ref[...] = weight_ref[0].astype(F32).T.astype(BF)


def ship_gradients(mine, halo_acc, hub_acc, grad_acc, wire_ref):
    rows = halo_acc[...].T.reshape(PEERS, SLOT, FIN)
    hubs = matmul(hub_acc[...].astype(BF), pick_hubs()).T.reshape(PEERS, 8, FIN)
    row = grad_acc[2 * FIN:2 * FIN + 1, :FIN]
    high = row.astype(BF).astype(F32)
    place = iota((8, FIN), 0)
    extra = jnp.where(place == 4, high, jnp.where(place == 5, row - high, 0.0))
    hubs = hubs + extra[None]
    right = jnp.concatenate([rows[:, 16:], hubs], axis=1)
    main = jnp.concatenate([rows[:, :16], right], axis=2)
    grads = pltpu.roll(grad_acc[:2 * FIN, :], mine * FIN, 1).reshape(16, 8, FOUT)
    grads = jnp.stack([grads[:, :, :LANES], grads[:, :, LANES:]], axis=1)
    grads = grads.reshape(32, 8, LANES)
    high = grads.astype(BF).astype(F32)
    low = grads - high
    swap = lambda x: jnp.concatenate([x[:, 4:], x[:, :4]], axis=1)
    first = iota((32, 8, LANES), 1) < 4
    even = jnp.where(first, high, swap(low))
    odd = jnp.where(first, swap(high), low)
    pieces = jnp.stack([even, odd], axis=1).reshape(PEERS, 8, LANES)
    wire = jnp.concatenate([main, pieces], axis=1)
    wire_ref[...] = wire.reshape(PEERS * WIDE, LANES).astype(BF)


def value_copies(part, bundles, value_ref, sems):
    own = pl.ds(STARTS[part], SIZES[part])
    return start_all(
        [(bundles[k].at[pl.ds(0, PACK), own], value_ref.at[k]) for k in range(FEATS)], sems
    )


def dense_half(
    part, means, value_ref, weight_ref, bias_ref, back_ref, index_ref, copies,
    halo_ref, hub_ref, out_ref, gmean_ref, ginput_ref, gpre_ref,
):
    chunk = CHUNK
    for i in range(SIZES[part] // chunk):
        here = slice(i * chunk, (i + 1) * chunk)
        whole = slice(STARTS[part] + i * chunk, STARTS[part] + (i + 1) * chunk)
        pre = jnp.tile(bias_ref[...], (1, chunk // LANES))
        for k in range(FEATS):
            both = jnp.concatenate([value_ref[k, :FIN, here], means[k][:, here]], axis=0)
            pre = pre + matmul(weight_ref[k], both).astype(BF).astype(F32)
        sigma = 0.5 * jnp.tanh(0.5 * pre) + 0.5
        out_ref[:, here] = (pre[:FIN] * sigma[:FIN]).astype(BF)
        slope = sigma * (1.0 + pre * (1.0 - sigma))
        gout = jnp.concatenate([value_ref[k, FIN:, here] for k in range(FEATS)], axis=0)
        gpre = (gout.astype(F32) * slope).astype(BF)
        gpre_ref[:, here] = gpre
        back = matmul(back_ref[...], gpre)
        ginput_ref[:, here] = back[:FIN]
        gmean_ref[:, here] = (back[FIN:] / index_ref[8:9, whole]).astype(BF)
    ones = jnp.ones((16, SIZES[part]), BF)
    left = jnp.concatenate([value_ref[0, :FIN], means[0][...], ones], axis=0)
    grads = matmul_nt(left, gpre_ref[...])
    for copy in copies:
        copy.wait()
    halos = matmul(gmean_ref[...], halo_ref[...])
    hubs = matmul(gmean_ref[...], hub_ref[...])
    return halos, hubs, grads


def first_dense_kernel(*refs):
    means, index_ref = refs[:4], refs[4]
    weight_ref, bias_ref, back_ref, value_ref = refs[5:9]
    bundles, halo_hbm, hub_hbm = refs[9:13], refs[13], refs[14]
    out_ref, gmean_ref, ginput_ref, halo_acc, hub_acc, grad_acc, later_ref = refs[15:22]
    gpre_ref, halo_ref, hub_ref, sems, later_sems = refs[22:]
    copies = adjacency_copies(STARTS[0], SIZES[0], 4, halo_hbm, hub_hbm, halo_ref, hub_ref, sems)
    later = value_copies(1, bundles, later_ref, later_sems)
    halo_acc[...], hub_acc[...], grad_acc[...] = dense_half(
        0, means, value_ref, weight_ref, bias_ref, back_ref, index_ref, copies,
        halo_ref, hub_ref, out_ref, gmean_ref, ginput_ref, gpre_ref,
    )
    for copy in later:
        copy.wait()


def later_dense_kernel(mine_ref, *refs):
    means, index_ref = refs[:4], refs[4]
    weight_ref, bias_ref, back_ref, value_ref = refs[5:9]
    held_halo, held_hub, held_grad, halo_hbm, hub_hbm = refs[9:14]
    out_ref, gmean_ref, ginput_ref, wire_ref = refs[14:18]
    gpre_ref, halo_ref, hub_ref, halo_acc, hub_acc, grad_acc, sems = refs[18:]
    copies = adjacency_copies(STARTS[1], SIZES[1], 4, halo_hbm, hub_hbm, halo_ref, hub_ref, sems)
    halos, hubs, grads = dense_half(
        1, means, value_ref, weight_ref, bias_ref, back_ref, index_ref, copies,
        halo_ref, hub_ref, out_ref, gmean_ref, ginput_ref, gpre_ref,
    )
    halo_acc[...] = held_halo[...] + halos
    hub_acc[...] = held_hub[...] + hubs
    grad_acc[...] = held_grad[...] + grads
    ship_gradients(mine_ref[0], halo_acc, hub_acc, grad_acc, wire_ref)


ACCUMULATORS = [(FIN, HALO), (FIN, HUB_ALL), (PACK + 16, FOUT)]
def halves(part):
    return [
        jax.ShapeDtypeStruct((FIN, SIZES[part]), BF),
        jax.ShapeDtypeStruct((FIN, SIZES[part]), BF),
        jax.ShapeDtypeStruct((FIN, SIZES[part]), F32),
    ]


def adjacency_scratch(part):
    return [
        pltpu.VMEM((FOUT, SIZES[part]), BF),
        pltpu.VMEM((SIZES[part], HALO), BF),
        pltpu.VMEM((SIZES[part], HUB_ALL), BF),
    ]


def first_dense(means, index, weights, value, bundles, halo_adj, hub_adj):
    out_shape = halves(0) + [pltpu.VMEM(shape, F32) for shape in ACCUMULATORS]
    out_shape += [pltpu.VMEM((FEATS, PACK, SIZES[1]), BF)]
    return pl.pallas_call(
        first_dense_kernel,
        in_specs=in_vmem(9) + [pl.BlockSpec(memory_space=pl.ANY)] + in_hbm(FEATS + 1),
        out_specs=in_vmem(len(out_shape)),
        out_shape=out_shape,
        scratch_shapes=adjacency_scratch(0)
        + [pltpu.SemaphoreType.DMA((5,)), pltpu.SemaphoreType.DMA((FEATS,))],
        compiler_params=params(),
        cost_estimate=cost(NODES * 2048 * 256, 6000000),
        name="dense",
    )(*means, index, *weights, value, bundles[0], *keep_hbm(*bundles[1:], halo_adj, hub_adj))


def later_dense(mine, means, index, weights, value, held, halo_adj, hub_adj):
    out_shape = halves(1) + [jax.ShapeDtypeStruct((PEERS * WIDE, LANES), BF)]
    return pl.pallas_call(
        later_dense_kernel,
        in_specs=[pl.BlockSpec(memory_space=pltpu.SMEM)] + in_vmem(12) + in_hbm(2),
        out_specs=in_vmem(len(out_shape)),
        out_shape=out_shape,
        scratch_shapes=adjacency_scratch(1)
        + [pltpu.VMEM(shape, F32) for shape in ACCUMULATORS]
        + [pltpu.SemaphoreType.DMA((5,))],
        compiler_params=params(),
        cost_estimate=cost(NODES * 2048 * 256, 6000000),
        name="dense",
    )(mine, *means, index, *weights, value, *held, *keep_hbm(halo_adj, hub_adj))


def back_kernel(
    ginput0, ginput1, gmean0, gmean1, out0, out1, adj_hbm, total_ref, out_ref, adj_ref, sems
):
    chunk = 256
    here = [pl.ds(i * chunk, chunk) for i in range(NODES // chunk)]
    blocks = start_all([(adj_hbm.at[:, i], adj_ref.at[:, i]) for i in here], sems)
    out_ref[:, :SIZES[0]] = out0[...]
    out_ref[:, SIZES[0]:] = out1[...]
    for i in range(NODES // chunk):
        blocks[i].wait()
        here = slice(i * chunk, (i + 1) * chunk)
        total = matmul(gmean0[...], adj_ref[:SIZES[0], here])
        total = total + matmul(gmean1[...], adj_ref[SIZES[0]:, here])
        half = ginput0 if i * chunk < SIZES[0] else ginput1
        start = i * chunk % SIZES[0]
        total_ref[:, here] = total + half[:, start:start + chunk]


def local_back(ginputs, gmeans, outs, adj):
    return pl.pallas_call(
        back_kernel,
        in_specs=in_vmem(6) + in_hbm(1),
        out_specs=in_vmem(2),
        out_shape=[
            pltpu.VMEM((FIN, NODES), F32),
            jax.ShapeDtypeStruct((FIN, NODES), BF),
        ],
        scratch_shapes=[
            pltpu.VMEM((NODES, NODES), BF),
            pltpu.SemaphoreType.DMA((8,)),
        ],
        compiler_params=params(),
        cost_estimate=cost(2 * NODES * NODES * 256, 10000000),
        name="local_back",
    )(*ginputs, *gmeans, *outs, *keep_hbm(adj))


def reduce_kernel(wire_ref, sums_ref, bias_ref):
    wire = wire_ref[...].astype(F32).reshape(PEERS, WIDE, LANES)
    pieces = jnp.sum(wire[:, 16:], axis=0)
    half = pieces[:4] + pieces[4:]
    both = jnp.concatenate([half, half], axis=0)
    sums_ref[...] = jnp.broadcast_to(both[None], (PEERS // 2, 8, LANES)).reshape(
        PEERS * 4, LANES
    )
    tail = jnp.sum(wire[:, 8:16], axis=0)
    bias_ref[...] = tail[4:5, FIN:] + tail[5:6, FIN:]


def reduce_grads(wire):
    return pl.pallas_call(
        reduce_kernel,
        out_shape=[
            jax.ShapeDtypeStruct((PEERS * 4, LANES), F32),
            jax.ShapeDtypeStruct((1, FIN), F32),
        ],
        compiler_params=params(),
        in_specs=in_vmem(1),
        out_specs=in_vmem(2),
        cost_estimate=cost(1000000, 1000000),
        name="reduce_grads",
    )(wire)


def scatter_kernel(wire_ref, index_ref, total_ref, out_ref):
    wire = wire_ref[...].astype(F32).reshape(PEERS, WIDE, LANES)
    both = wire[:, :16].reshape(SLOTS, LANES).T
    back = jnp.concatenate([both[:FIN], both[FIN:]], axis=1).astype(BF)
    chunk = 256
    target = index_ref[0:1, :].astype(I32)
    node = iota((chunk, 2 * SLOTS), 0)
    for k in range(NODES // chunk):
        here = slice(k * chunk, (k + 1) * chunk)
        hot = (node == target - k * chunk).astype(F32).astype(BF)
        out_ref[:, here] = (total_ref[:, here] + matmul_nt(back, hot)).astype(BF)


def scatter_rows(wire, index, total):
    return pl.pallas_call(
        scatter_kernel,
        in_specs=in_vmem(3),
        out_specs=in_vmem(1)[0],
        out_shape=jax.ShapeDtypeStruct((FIN, NODES), BF),
        compiler_params=params(),
        cost_estimate=cost(2 * 2 * SLOTS * NODES * 256, 2000000),
        name="scatter_rows",
    )(wire, index, total)


def from_feat(value):
    shifted = [
        lax.ppermute(value, "feat", [(j, (j - k) % FEATS) for j in range(FEATS)])
        for k in range(1, FEATS)
    ]
    return [value] + shifted


def on_device(
    features,
    w_self,
    w_neigh,
    bias,
    grad_out,
    degree,
    tiles,
    tile_src,
    tile_dst,
    tile_count,
    halo_adj,
    send_rows,
    send_count,
    hub_adj,
    hub_local,
):
    feat = features.T
    gout = grad_out.T
    mine = lax.axis_index("feat").astype(I32).reshape(1)
    degree = degree.reshape(1, NODES)
    send = jnp.transpose(send_rows[0])
    packed = bundle(feat, gout, w_self, w_neigh, bias.reshape(1, FIN))
    packed, feat = lax.optimization_barrier((packed, feat))
    bundles = from_feat(packed)
    wire, index = gather_rows(hub_local, send, send_count, feat, degree)
    arrived = lax.all_to_all(wire, "dom", split_axis=0, concat_axis=0, tiled=True)
    local, adj = local_sum(tile_src, tile_dst, tile_count, tiles, feat)
    mean, *known = first_mean(arrived, halo_adj, hub_adj, local, index)
    mean, bundles = lax.optimization_barrier((mean, bundles))
    first = from_feat(mean)
    mean, *weights, value = later_mean(
        mine, known, local, index, halo_adj, hub_adj, bundles
    )
    second = from_feat(mean)
    out0, gmean0, ginput0, *held, value = first_dense(
        first, index, weights, value, bundles, halo_adj, hub_adj
    )
    out1, gmean1, ginput1, wire = later_dense(
        mine, second, index, weights, value, held, halo_adj, hub_adj
    )
    returned = lax.all_to_all(wire, "dom", split_axis=0, concat_axis=0, tiled=True)
    total, out = local_back([ginput0, ginput1], [gmean0, gmean1], [out0, out1], adj)
    returned, total = lax.optimization_barrier((returned, total))
    sums, grad_bias = reduce_grads(returned)
    shared = lax.all_to_all(sums, "dom", split_axis=0, concat_axis=0, tiled=True)
    grad_features = scatter_rows(returned, index, total)
    grads = shared.reshape(16, 2, 8, LANES).transpose(0, 2, 1, 3).reshape(PACK, FOUT)
    return (
        out.T,
        grad_features.T,
        grads[:FIN],
        grads[FIN:],
        grad_bias.reshape(FIN),
    )


def solution(mesh):
    in_specs = (
        P("dom", "feat"),
        P("feat", None),
        P("feat", None),
        P("feat"),
        P("dom", "feat"),
        P("dom"),
        P("dom", None, None),
        P("dom"),
        P("dom"),
        P("dom"),
        P("dom", None),
        P("dom", None, None),
        P("dom", None),
        P("dom", None),
        P("dom"),
    )
    out_specs = (P("dom", "feat"), P("dom", "feat"), P("feat", None), P("feat", None), P("feat"))
    return jax.shard_map(
        on_device, mesh=mesh, in_specs=in_specs, out_specs=out_specs, check_vma=False
    )
```
